32 devices in a mesh: path: 8 (over z, y), dim: 4 (over x, core).
Axes of the slice: x: 2, y: 2, z: 4, core: 2. Of those that a mesh axis runs over, the one named last changes fastest.
Arguments:
- inner_noise: bfloat16 [64, 1000, 512], P('path', 'dim'), may hold values from -6 to 6
- outer_noise: bfloat16 [1000, 512], P('dim'), may hold values from -6 to 6
- start: float32 [1000], P('dim'), may hold values from 0.8 to 1.25
- vol: float32 [1000], P('dim'), may hold values from 0.1 to 0.4
- times: float32 [512], replicated, may hold values from 0.1 to 0.9
Outputs:
- root_value: float32 [1], replicated
- root_grad: float32 [1000], P('dim')
- point_value: float32 [512], P('path')
- point_grad: float32 [1000, 512], P('dim', 'path')
The draws below stay inside these ranges and needn't reach their ends.
All inputs are finite; a program needn't handle non-finite values.
Results may differ from the reference program's by a relative error of at most 0.0003.
Values sent between devices are 32-bit elements; how exact they have to be, the bound alone decides.
No kernel may reach another device: no remote copies, remote signals or barrier semaphores. Data moves between devices by JAX's collectives and lax.ppermute only.
A program may use at most 64 MiB of HBM per device.

```python
import math
import jax
import jax.numpy as jnp
from jax import lax

D = 1000
M = 512
K = 64


def shard_levels(rng, shape, split, low, high):
    gain = 1.0
    for dim, blocks in split:
        steps = jax.random.uniform(jax.random.fold_in(jax.random.fold_in(rng, 6), dim), (blocks,), jnp.float32, low / len(split), high / len(split))
        gain = gain * jnp.repeat(jnp.exp(steps), shape[dim] // blocks).reshape((-1,) + (1,) * (len(shape) - 1 - dim))
    return gain


def centred(own_key, shape, width, most, pieces=(), held_as=jnp.bfloat16):
    factor_of = shard_levels(own_key, shape, pieces, -0.22, 0.18) if pieces else 1.0
    result = jax.random.normal(own_key, shape, jnp.float32) * width * factor_of
    return jnp.minimum(jnp.maximum(result, -most), most).astype(held_as)


def setup_inputs(seed: int = 0) -> dict:
    key_list = jax.random.split(jax.random.key(seed), 6)
    return {
        "inner_noise": centred(key_list[0], (K, D, M), 1.0, 6.0, ((0, 8), (1, 4))),
        "outer_noise": centred(key_list[1], (D, M), 1.0, 6.0, ((0, 4),)),
        "start": jnp.clip(jnp.exp(math.log(1.25) - 0.4462871 * jax.random.uniform(key_list[2], (D,), jnp.float32) ** shard_levels(key_list[2], (D,), ((0, 4),), -0.2, 0.2)), 0.8, 1.25),
        "vol": jnp.clip(jnp.exp(math.log(0.4) - 1.3862944 * jax.random.uniform(key_list[3], (D,), jnp.float32) ** shard_levels(key_list[3], (D,), ((0, 4),), -0.2, 0.2)), 0.1, 0.4),
        "times": jnp.clip(jax.random.uniform(key_list[4], (M,), jnp.float32, 0.1, 0.9), 0.1, 0.9),
    }


drift = 0.02
delta = 2.0 / 3.0
rate_free = 0.02
gamma_high = 0.2
gamma_low = 0.02
value_high = 0.4
value_low = 0.7

def driver_of(value):
    slope = jnp.clip((value - value_high) / (value_low - value_high), 0.0, 1.0)
    quota = gamma_high + (gamma_low - gamma_high) * slope
    return -(1.0 - delta) * quota * value - rate_free * value

def reference(inner_noise, outer_noise, start, vol, times):
    tau = 1.0 - times
    outer = outer_noise.astype(jnp.float32)
    mean_rate = (drift - 0.5 * vol * vol)[:, None]
    outer_state = start[:, None] * jnp.exp(mean_rate * times[None, :] + vol[:, None] * jnp.sqrt(times)[None, :] * outer)
    inner_drift = mean_rate * tau[None, :]
    inner_scale = vol[:, None] * jnp.sqrt(tau)[None, :]

    def one_path(carry, noise):
        totals, moments = carry
        shock = noise.astype(jnp.float32)
        level = outer_state * jnp.exp(inner_drift + inner_scale * shock)
        payoff = lax.optimization_barrier(jnp.min(level, axis=0))
        return ((totals + payoff, moments + payoff[None, :] * shock), None)
    init = (jnp.zeros((M,), jnp.float32), jnp.zeros((D, M), jnp.float32))
    (totals, moments), _ = lax.scan(one_path, init, inner_noise)
    point_value = totals / K
    point_grad = moments / (K * vol[:, None] * outer_state * jnp.sqrt(tau)[None, :])
    driver = driver_of(point_value)
    root_value = jnp.sum(totals) / (M * K) + jnp.sum(driver) / M
    terminal = lax.optimization_barrier(jnp.sum(jnp.sqrt(times)[None, :] * outer * totals[None, :] + jnp.sqrt(tau)[None, :] * moments, axis=1))
    integral = lax.optimization_barrier(jnp.sum(driver[None, :] * outer / jnp.sqrt(times)[None, :], axis=1))
    root_grad = terminal / (M * K * vol * start) + integral / (M * vol * start)
    return (jnp.reshape(root_value, (1,)), root_grad, point_value, point_grad)
```

```python
import functools

import jax
import jax.numpy as jnp
from jax import lax
from jax.experimental import pallas as pl
from jax.experimental.pallas import tpu as pltpu
from jax.sharding import PartitionSpec as P

drift = 0.02
delta = 2.0 / 3.0
rate_free = 0.02
gamma_high = 0.2
gamma_low = 0.02
value_high = 0.4
value_low = 0.7

LANES = 128
HALF = LANES // 2
EXTRA = 8
F32 = jnp.float32


def driver_of(value):
    slope = jnp.clip((value - value_high) / (value_low - value_high), 0.0, 1.0)
    quota = gamma_high + (gamma_low - gamma_high) * slope
    return -(1.0 - delta) * quota * value - rate_free * value


def is_power(n):
    return n > 0 and n & (n - 1) == 0


def general(inner_noise, outer_noise, start, vol, times):
    paths_here = inner_noise.shape[0]
    points = times.shape[0]
    groups = lax.axis_size("path")
    inner_total = paths_here * groups
    owned = points // groups
    tau = 1.0 - times
    outer = outer_noise.astype(F32)
    mean_rate = (drift - 0.5 * vol * vol)[:, None]
    outer_state = start[:, None] * jnp.exp(
        mean_rate * times[None, :] + vol[:, None] * jnp.sqrt(times)[None, :] * outer
    )
    shock = inner_noise.astype(F32)
    level = outer_state[None] * jnp.exp(
        (mean_rate * tau[None, :])[None] + (vol[:, None] * jnp.sqrt(tau)[None, :])[None] * shock
    )
    payoff = lax.pmin(jnp.min(level, axis=1), "dim")
    totals = jnp.sum(payoff, axis=0)
    moments = jnp.sum(payoff[:, None, :] * shock, axis=0)
    start_index = lax.axis_index("path") * owned
    totals, moments = lax.psum((totals, moments), "path")
    point_value = totals / inner_total
    point_grad_all = moments / (inner_total * vol[:, None] * outer_state * jnp.sqrt(tau)[None, :])
    driver = driver_of(point_value)
    root_value = jnp.sum(totals) / (points * inner_total) + jnp.sum(driver) / points
    terminal = jnp.sum(
        jnp.sqrt(times)[None, :] * outer * totals[None, :] + jnp.sqrt(tau)[None, :] * moments,
        axis=1,
    )
    integral = jnp.sum(driver[None, :] * outer / jnp.sqrt(times)[None, :], axis=1)
    root_grad = terminal / (points * inner_total * vol * start) + integral / (points * vol * start)
    own_value = lax.dynamic_slice_in_dim(point_value, start_index, owned, 0)
    own_grad = lax.dynamic_slice_in_dim(point_grad_all, start_index, owned, 1)
    return (jnp.reshape(root_value, (1,)), root_grad, own_value, own_grad)


def row_tiles(rows):
    return [(r, min(16, rows - r)) for r in range(0, rows, 16)]


def as_columns(row, rows):
    full = -(-rows // LANES) * LANES
    row = jnp.concatenate([row, jnp.ones((1, full - rows), F32)], axis=1)
    return jnp.transpose(jnp.broadcast_to(row, (8, full)))[:, 0:1]


def swap_halves(block):
    return pltpu.roll(block, HALF, 1)


def low_lanes(shape):
    return lax.broadcasted_iota(jnp.int32, shape, 1) < HALF


def pack_low(top, bottom):
    return jnp.where(low_lanes(top.shape), top, swap_halves(bottom))


def pack_high(top, bottom):
    return jnp.where(low_lanes(top.shape), swap_halves(top), bottom)


def minima_kernel(noise_hbm, outer_ref, start_ref, vol_ref, times_ref, out_ref, noise_v, sems):
    paths, rows, points = noise_hbm.shape
    copies = [
        pltpu.make_async_copy(noise_hbm.at[k], noise_v.at[k], sems.at[k]) for k in range(paths)
    ]
    for c in copies:
        c.start()
    vol_row = vol_ref[...]
    base = as_columns(jnp.log(start_ref[...]) + (drift - 0.5 * vol_row * vol_row), rows)
    vol = as_columns(vol_row, rows)
    times = times_ref[...]
    root_times = jnp.sqrt(times)
    root_tau = jnp.sqrt(1.0 - times)
    for c in copies:
        c.wait()
    low = None
    for r, n in row_tiles(rows):
        v = vol[r : r + n]
        a = base[r : r + n] + (v * root_times) * outer_ref[r : r + n, :].astype(F32)
        b = v * root_tau
        here = []
        for k in range(paths):
            level = a + b * noise_v[k, r : r + n, :].astype(F32)
            if n == 16:
                here.append(jnp.minimum(level[0:8], level[8:16]))
            else:
                least = jnp.min(level, axis=0, keepdims=True)
                here.append(jnp.broadcast_to(least, (8, points)))
        low = here if low is None else [jnp.minimum(p, q) for p, q in zip(low, here)]
    for k in range(paths):
        out_ref[k : k + 1, :] = jnp.min(low[k], axis=0, keepdims=True)


def moments_kernel(
    zs, l0, l1, l2, l3, noise_ref, times_ref, send_far, keep_far, send_near, keep_near, pay, term
):
    paths, rows, points = noise_ref.shape
    me = lax.axis_index("path")
    z = me // 2
    first = me % 2 == 0
    payoff = jnp.exp(jnp.minimum(jnp.minimum(l0[...], l1[...]), jnp.minimum(l2[...], l3[...])))
    pay[...] = payoff
    totals = jnp.sum(payoff, axis=0, keepdims=True)
    half = zs // 2
    for step in range(zs):
        s = zs - 1 - step
        send, keep = (send_far, keep_far) if s >= half else (send_near, keep_near)
        place = (step if s >= half else step - half) * LANES
        columns = pl.ds(pl.multiple_of((z ^ s) * LANES, LANES), LANES)
        weights = [pay[k : k + 1, columns] for k in range(paths)]
        root_tau = jnp.sqrt(1.0 - times_ref[0:1, columns])

        def tile(r):
            n = min(16, rows - r)
            if n <= 0:
                return jnp.zeros((16, LANES), F32)
            total = weights[0] * noise_ref[0, r : r + n, columns].astype(F32)
            for k in range(1, paths):
                total = total + weights[k] * noise_ref[k, r : r + n, columns].astype(F32)
            if n < 16:
                total = jnp.concatenate([total, jnp.zeros((16 - n, LANES), F32)], axis=0)
            return total

        for r in range(0, LANES, 16):
            top, bottom = tile(r), tile(LANES + r)
            low, high = pack_low(top, bottom), pack_high(top, bottom)
            send[place + r : place + r + 16, :] = jnp.where(first, high, low)
            keep[place + r : place + r + 16, :] = jnp.where(first, low, high)
            for at, part in ((r, top), (LANES + r, bottom)):
                if step == 0:
                    term[at : at + 16, :] = root_tau * part
                else:
                    term[at : at + 16, :] += root_tau * part
    tail = half * LANES
    extras = [totals[:, c : c + LANES] for c in range(0, points, LANES)]
    for r in (0, LANES):
        extras.append(jnp.sum(jnp.transpose(term[r : r + LANES, :]), axis=0, keepdims=True))
    extras.append(jnp.zeros((EXTRA - len(extras), LANES), F32))
    extras = jnp.concatenate(extras, axis=0)
    send_far[tail : tail + EXTRA, :] = extras
    keep_far[tail : tail + EXTRA, :] = extras


def scale_kernel(inner_total, outer_ref, start_ref, vol_ref, times_ref, out_ref):
    rows = outer_ref.shape[0]
    me = lax.axis_index("path")
    z = me // 2
    first = me % 2 == 0
    columns = pl.ds(pl.multiple_of(z * LANES, LANES), LANES)

    def pack(top, bottom):
        return jnp.where(first, pack_low(top, bottom), pack_high(top, bottom))

    vol = as_columns(vol_ref[...], rows)
    start = as_columns(start_ref[...], rows)
    spare = jnp.zeros((2 * LANES - rows, LANES), F32)
    outer = outer_ref[:, columns].astype(F32)
    outer = pack(outer[0:LANES], jnp.concatenate([outer[LANES:rows], spare], axis=0))
    times = times_ref[0:1, columns]
    times = pack(times, times)
    side = low_lanes((LANES, LANES))
    vol = jnp.where(side, vol[0:LANES], vol[LANES:])
    start = jnp.where(side, start[0:LANES], start[LANES:])
    state = start * jnp.exp((drift - 0.5 * vol * vol) * times + vol * jnp.sqrt(times) * outer)
    out_ref[...] = 1.0 / (inner_total * vol * state * jnp.sqrt(1.0 - times))


def final_kernel(
    inner_total, n_parts, own_ref, extra_ref, scale_ref, outer_ref, start_ref, vol_ref, times_ref, *rest
):
    parts, (value_ref, grad_ref, point_ref, point_grad_ref) = rest[:n_parts], rest[n_parts:]
    rows, points = outer_ref.shape
    me = lax.axis_index("path")
    first = me % 2 == 0
    moments = own_ref[...]
    extra = extra_ref[...]
    for part in parts:
        moments = moments + part[0:LANES, :]
        extra = extra + part[LANES : LANES + EXTRA, :]
    grad = moments * scale_ref[...]
    point_grad_ref[0:LANES, :] = grad[:, 0:HALF]
    point_grad_ref[LANES:rows, :] = swap_halves(grad)[0 : rows - LANES, 0:HALF]
    blocks = points // LANES
    totals = jnp.concatenate([extra[c : c + 1, :] for c in range(blocks)], axis=1)
    inner_term = jnp.concatenate([extra[blocks : blocks + 1, :], extra[blocks + 1 : blocks + 2, :]], axis=1)
    values = totals / inner_total
    driver = driver_of(values)
    value_ref[...] = jnp.sum(totals, axis=1, keepdims=True) / (points * inner_total) + (
        jnp.sum(driver, axis=1, keepdims=True) / points
    )
    own = extra[0:1, :]
    for c in range(1, blocks):
        own = jnp.where(me // 2 == c, extra[c : c + 1, :], own)
    own = jnp.where(first, own, swap_halves(own)) / inner_total
    point_ref[...] = own[:, 0:HALF]
    root_times = jnp.sqrt(times_ref[...])
    weight = totals * root_times / inner_total + driver / root_times
    outer_term = lax.dot_general(
        jnp.broadcast_to(weight, (8, points)),
        outer_ref[...].astype(F32),
        (((1,), (1,)), ((), ())),
        precision=lax.Precision.HIGHEST,
        preferred_element_type=F32,
    )[0:1, :]
    grad_ref[...] = (inner_term[:, 0:rows] / inner_total + outer_term) / (
        points * vol_ref[...] * start_ref[...]
    )


def paired(inner_noise, outer_noise, start, vol, times):
    paths, rows, points = inner_noise.shape
    groups, dims = lax.axis_size("path"), lax.axis_size("dim")
    inner_total = paths * groups
    zs = groups // 2
    half = zs // 2
    start_row, vol_row, times_row = start[None, :], vol[None, :], times[None, :]
    limit = pltpu.CompilerParams(vmem_limit_bytes=16 * 1024 * 1024)

    lows = pl.pallas_call(
        minima_kernel,
        out_shape=jax.ShapeDtypeStruct((paths, points), F32),
        in_specs=[pl.BlockSpec(memory_space=pl.ANY)] + [pl.BlockSpec()] * 4,
        scratch_shapes=[
            pltpu.VMEM((paths, rows, points), inner_noise.dtype),
            pltpu.SemaphoreType.DMA((paths,)),
        ],
        compiler_params=limit,
        name="minima",
    )(inner_noise, outer_noise, start_row, vol_row, times_row)

    others = [
        lax.ppermute(lows, "dim", [(i, i ^ s) for i in range(dims)]) for s in range(1, dims)
    ]
    shapes = [half * LANES + EXTRA] * 2 + [half * LANES] * 2
    send_far, keep_far, send_near, keep_near = pl.pallas_call(
        functools.partial(moments_kernel, zs),
        out_shape=[jax.ShapeDtypeStruct((n, LANES), F32) for n in shapes],
        scratch_shapes=[pltpu.VMEM((paths, points), F32), pltpu.VMEM((2 * LANES, LANES), F32)],
        compiler_params=limit,
        name="moments",
    )(lows, *others, inner_noise, times_row)

    swap = [(i, i ^ 1) for i in range(groups)]
    far = keep_far + lax.ppermute(send_far, "path", swap)
    near = keep_near + lax.ppermute(send_near, "path", swap)
    scale = pl.pallas_call(
        functools.partial(scale_kernel, inner_total),
        out_shape=jax.ShapeDtypeStruct((LANES, LANES), F32),
        compiler_params=limit,
        name="scale",
    )(outer_noise, start_row, vol_row, times_row)
    extra = far[half * LANES :]
    arrived = []
    for step in range(zs - 1):
        s = zs - 1 - step
        held, at = (far, step) if s >= half else (near, step - half)
        message = jnp.concatenate([held[at * LANES : (at + 1) * LANES], extra], axis=0)
        arrived.append(lax.ppermute(message, "path", [(i, i ^ (2 * s)) for i in range(groups)]))
    own = near[(half - 1) * LANES :]

    value, grad, point, point_grad = pl.pallas_call(
        functools.partial(final_kernel, inner_total, len(arrived)),
        out_shape=[
            jax.ShapeDtypeStruct((1, 1), F32),
            jax.ShapeDtypeStruct((1, rows), F32),
            jax.ShapeDtypeStruct((1, points // groups), F32),
            jax.ShapeDtypeStruct((rows, points // groups), F32),
        ],
        compiler_params=limit,
        name="final",
    )(own, extra, scale, outer_noise, start_row, vol_row, times_row, *arrived)
    return value.reshape(1), grad.reshape(rows), point.reshape(points // groups), point_grad


def per_device(inner_noise, outer_noise, start, vol, times):
    rows, points = outer_noise.shape
    groups, dims = lax.axis_size("path"), lax.axis_size("dim")
    fits = (
        2 * points == LANES * groups
        and LANES < rows <= 2 * LANES
        and is_power(groups)
        and groups >= 4
        and dims == 4
        and points // LANES + 2 <= EXTRA
    )
    return (paired if fits else general)(inner_noise, outer_noise, start, vol, times)


def solution(mesh):
    in_specs = (P("path", "dim", None), P("dim", None), P("dim"), P("dim"), P())
    out_specs = (P(), P("dim"), P("path"), P("dim", "path"))
    return jax.shard_map(
        per_device, mesh=mesh, in_specs=in_specs, out_specs=out_specs, check_vma=False
    )
```

```python
import functools

import jax
import jax.numpy as jnp
from jax import lax
from jax.experimental import pallas as pl
from jax.experimental.pallas import tpu as pltpu
from jax.sharding import PartitionSpec as P

drift = 0.02
delta = 2.0 / 3.0
rate_free = 0.02
gamma_high = 0.2
gamma_low = 0.02
value_high = 0.4
value_low = 0.7

LANES = 128
HALF = LANES // 2
EXTRA = 8
CHUNKS = 4
STEP = 8
F32 = jnp.float32


def driver_of(value):
    slope = jnp.clip((value - value_high) / (value_low - value_high), 0.0, 1.0)
    quota = gamma_high + (gamma_low - gamma_high) * slope
    return -(1.0 - delta) * quota * value - rate_free * value


def is_power(n):
    return n > 0 and n & (n - 1) == 0


def general(inner_noise, outer_noise, start, vol, times):
    paths_here = inner_noise.shape[0]
    points = times.shape[0]
    groups = lax.axis_size("path")
    inner_total = paths_here * groups
    owned = points // groups
    tau = 1.0 - times
    outer = outer_noise.astype(F32)
    mean_rate = (drift - 0.5 * vol * vol)[:, None]
    outer_state = start[:, None] * jnp.exp(
        mean_rate * times[None, :] + vol[:, None] * jnp.sqrt(times)[None, :] * outer
    )
    shock = inner_noise.astype(F32)
    level = outer_state[None] * jnp.exp(
        (mean_rate * tau[None, :])[None] + (vol[:, None] * jnp.sqrt(tau)[None, :])[None] * shock
    )
    payoff = lax.pmin(jnp.min(level, axis=1), "dim")
    totals = jnp.sum(payoff, axis=0)
    moments = jnp.sum(payoff[:, None, :] * shock, axis=0)
    start_index = lax.axis_index("path") * owned
    totals, moments = lax.psum((totals, moments), "path")
    point_value = totals / inner_total
    point_grad_all = moments / (inner_total * vol[:, None] * outer_state * jnp.sqrt(tau)[None, :])
    driver = driver_of(point_value)
    root_value = jnp.sum(totals) / (points * inner_total) + jnp.sum(driver) / points
    terminal = jnp.sum(
        jnp.sqrt(times)[None, :] * outer * totals[None, :] + jnp.sqrt(tau)[None, :] * moments,
        axis=1,
    )
    integral = jnp.sum(driver[None, :] * outer / jnp.sqrt(times)[None, :], axis=1)
    root_grad = terminal / (points * inner_total * vol * start) + integral / (points * vol * start)
    own_value = lax.dynamic_slice_in_dim(point_value, start_index, owned, 0)
    own_grad = lax.dynamic_slice_in_dim(point_grad_all, start_index, owned, 1)
    return (jnp.reshape(root_value, (1,)), root_grad, own_value, own_grad)


def row_tiles(rows):
    return [(r, min(16, rows - r)) for r in range(0, rows, 16)]


def as_columns(row, rows):
    full = -(-rows // LANES) * LANES
    row = jnp.concatenate([row, jnp.ones((1, full - rows), F32)], axis=1)
    return jnp.transpose(jnp.broadcast_to(row, (8, full)))[:, 0:1]


def swap_halves(block):
    return pltpu.roll(block, HALF, 1)


def low_lanes(shape):
    return lax.broadcasted_iota(jnp.int32, shape, 1) < HALF


def pack_low(top, bottom):
    return jnp.where(low_lanes(top.shape), top, swap_halves(bottom))


def pack_high(top, bottom):
    return jnp.where(low_lanes(top.shape), swap_halves(top), bottom)


def minima_kernel(
    noise_hbm, outer_hbm, start_hbm, vol_hbm, times_hbm, out_ref, noise_v,
    outer_ref, start_ref, vol_ref, times_ref, level_v, slope_v, sems,
):
    rows, paths, points = noise_hbm.shape
    cuts = [rows * c // CHUNKS // 16 * 16 for c in range(CHUNKS)] + [rows]
    spans = list(zip(cuts[:-1], cuts[1:]))
    copies = [
        pltpu.make_async_copy(noise_hbm.at[lo:hi], noise_v.at[lo:hi], sems.at[c])
        for c, (lo, hi) in enumerate(spans)
    ]
    small = [
        pltpu.make_async_copy(src, dst, sems.at[CHUNKS + c])
        for c, (src, dst) in enumerate(
            [(vol_hbm, vol_ref), (start_hbm, start_ref), (times_hbm, times_ref), (outer_hbm, outer_ref)]
        )
    ]
    for c in small + copies:
        c.start()
    for c in small[:3]:
        c.wait()
    vol_row = vol_ref[...]
    base = as_columns(jnp.log(start_ref[...]) + (drift - 0.5 * vol_row * vol_row), rows)
    vol = as_columns(vol_row, rows)
    times = times_ref[...]
    root_times = jnp.sqrt(times)
    root_tau = jnp.sqrt(1.0 - times)
    small[3].wait()
    for r, n in row_tiles(rows):
        v = vol[r : r + n]
        level_v[r : r + n, :] = base[r : r + n] + (v * root_times) * outer_ref[r : r + n, :].astype(F32)
        slope_v[r : r + n, :] = v * root_tau

    def level(d):
        shock = noise_v[d].astype(F32)
        return level_v[pl.ds(d, 1), :] + slope_v[pl.ds(d, 1), :] * shock

    low = jnp.full((paths, points), jnp.inf, F32)
    for (lo, hi), c in zip(spans, copies):
        c.wait()
        size = hi - lo
        whole = size // STEP

        def body(t, low, lo=lo):
            for j in range(STEP):
                low = jnp.minimum(low, level(lo + t * STEP + j))
            return low

        low = lax.fori_loop(0, whole, body, low)
        for d in range(lo + whole * STEP, hi):
            low = jnp.minimum(low, level(d))
    out_ref[...] = low


def moments_kernel(
    zs, l0, l1, l2, l3, noise_ref, times_ref, send_far, keep_far, send_near, keep_near, pay, term
):
    paths, rows, points = noise_ref.shape
    me = lax.axis_index("path")
    z = me // 2
    first = me % 2 == 0
    payoff = jnp.exp(jnp.minimum(jnp.minimum(l0[...], l1[...]), jnp.minimum(l2[...], l3[...])))
    pay[...] = payoff
    totals = jnp.sum(payoff, axis=0, keepdims=True)
    half = zs // 2
    for step in range(zs):
        s = zs - 1 - step
        send, keep = (send_far, keep_far) if s >= half else (send_near, keep_near)
        place = (step if s >= half else step - half) * LANES
        columns = pl.ds(pl.multiple_of((z ^ s) * LANES, LANES), LANES)
        weights = [pay[k : k + 1, columns] for k in range(paths)]
        root_tau = jnp.sqrt(1.0 - times_ref[0:1, columns])

        def tile(r):
            n = min(16, rows - r)
            if n <= 0:
                return jnp.zeros((16, LANES), F32)
            total = weights[0] * noise_ref[0, r : r + n, columns].astype(F32)
            for k in range(1, paths):
                total = total + weights[k] * noise_ref[k, r : r + n, columns].astype(F32)
            if n < 16:
                total = jnp.concatenate([total, jnp.zeros((16 - n, LANES), F32)], axis=0)
            return total

        for r in range(0, LANES, 16):
            top, bottom = tile(r), tile(LANES + r)
            low, high = pack_low(top, bottom), pack_high(top, bottom)
            send[place + r : place + r + 16, :] = jnp.where(first, high, low)
            keep[place + r : place + r + 16, :] = jnp.where(first, low, high)
            for at, part in ((r, top), (LANES + r, bottom)):
                if step == 0:
                    term[at : at + 16, :] = root_tau * part
                else:
                    term[at : at + 16, :] += root_tau * part
    tail = half * LANES
    extras = [totals[:, c : c + LANES] for c in range(0, points, LANES)]
    for r in (0, LANES):
        extras.append(jnp.sum(jnp.transpose(term[r : r + LANES, :]), axis=0, keepdims=True))
    extras.append(jnp.zeros((EXTRA - len(extras), LANES), F32))
    extras = jnp.concatenate(extras, axis=0)
    send_far[tail : tail + EXTRA, :] = extras
    keep_far[tail : tail + EXTRA, :] = extras


def scale_kernel(inner_total, outer_ref, start_ref, vol_ref, times_ref, out_ref):
    rows = outer_ref.shape[0]
    me = lax.axis_index("path")
    z = me // 2
    first = me % 2 == 0
    columns = pl.ds(pl.multiple_of(z * LANES, LANES), LANES)

    def pack(top, bottom):
        return jnp.where(first, pack_low(top, bottom), pack_high(top, bottom))

    vol = as_columns(vol_ref[...], rows)
    start = as_columns(start_ref[...], rows)
    spare = jnp.zeros((2 * LANES - rows, LANES), F32)
    outer = outer_ref[:, columns].astype(F32)
    outer = pack(outer[0:LANES], jnp.concatenate([outer[LANES:rows], spare], axis=0))
    times = times_ref[0:1, columns]
    times = pack(times, times)
    side = low_lanes((LANES, LANES))
    vol = jnp.where(side, vol[0:LANES], vol[LANES:])
    start = jnp.where(side, start[0:LANES], start[LANES:])
    state = start * jnp.exp((drift - 0.5 * vol * vol) * times + vol * jnp.sqrt(times) * outer)
    out_ref[...] = 1.0 / (inner_total * vol * state * jnp.sqrt(1.0 - times))


def final_kernel(
    inner_total, n_parts, own_ref, extra_ref, scale_ref, outer_ref, start_ref, vol_ref, times_ref, *rest
):
    parts, (value_ref, grad_ref, point_ref, point_grad_ref) = rest[:n_parts], rest[n_parts:]
    rows, points = outer_ref.shape
    me = lax.axis_index("path")
    first = me % 2 == 0
    moments = own_ref[...]
    extra = extra_ref[...]
    for part in parts:
        moments = moments + part[0:LANES, :]
        extra = extra + part[LANES : LANES + EXTRA, :]
    grad = moments * scale_ref[...]
    turned = jnp.transpose(grad)
    point_grad_ref[:, 0:LANES] = turned[0:HALF]
    point_grad_ref[:, LANES:rows] = turned[HALF:, 0 : rows - LANES]
    blocks = points // LANES
    totals = jnp.concatenate([extra[c : c + 1, :] for c in range(blocks)], axis=1)
    inner_term = jnp.concatenate([extra[blocks : blocks + 1, :], extra[blocks + 1 : blocks + 2, :]], axis=1)
    values = totals / inner_total
    driver = driver_of(values)
    value_ref[...] = jnp.sum(totals, axis=1, keepdims=True) / (points * inner_total) + (
        jnp.sum(driver, axis=1, keepdims=True) / points
    )
    own = extra[0:1, :]
    for c in range(1, blocks):
        own = jnp.where(me // 2 == c, extra[c : c + 1, :], own)
    own = jnp.where(first, own, swap_halves(own)) / inner_total
    point_ref[...] = own[:, 0:HALF]
    root_times = jnp.sqrt(times_ref[...])
    weight = totals * root_times / inner_total + driver / root_times
    outer_term = lax.dot_general(
        jnp.broadcast_to(weight, (8, points)),
        outer_ref[...].astype(F32),
        (((1,), (1,)), ((), ())),
        precision=lax.Precision.HIGHEST,
        preferred_element_type=F32,
    )[0:1, :]
    grad_ref[...] = (inner_term[:, 0:rows] / inner_total + outer_term) / (
        points * vol_ref[...] * start_ref[...]
    )


def paired(inner_noise, outer_noise, start, vol, times):
    paths, rows, points = inner_noise.shape
    groups, dims = lax.axis_size("path"), lax.axis_size("dim")
    inner_total = paths * groups
    zs = groups // 2
    half = zs // 2
    start_row, vol_row, times_row = start[None, :], vol[None, :], times[None, :]
    limit = pltpu.CompilerParams(vmem_limit_bytes=16 * 1024 * 1024)

    lows, held_noise = pl.pallas_call(
        minima_kernel,
        out_shape=(
            pltpu.VMEM((paths, points), F32),
            pltpu.VMEM((rows, paths, points), inner_noise.dtype),
        ),
        in_specs=[pl.BlockSpec(memory_space=pltpu.HBM)] * 5,
        scratch_shapes=[
            pltpu.VMEM((rows, points), outer_noise.dtype),
            pltpu.VMEM((1, rows), F32),
            pltpu.VMEM((1, rows), F32),
            pltpu.VMEM((1, points), F32),
            pltpu.VMEM((rows, points), F32),
            pltpu.VMEM((rows, points), F32),
            pltpu.SemaphoreType.DMA((CHUNKS + 4,)),
        ],
        compiler_params=limit,
        name="minima",
    )(*[
        pltpu.with_memory_space_constraint(x, pltpu.HBM)
        for x in (jnp.transpose(inner_noise, (1, 0, 2)), outer_noise, start_row, vol_row, times_row)
    ])
    held_noise = jnp.transpose(held_noise, (1, 0, 2))

    others = [
        lax.ppermute(lows, "dim", [(i, i ^ s) for i in range(dims)]) for s in range(1, dims)
    ]
    shapes = [half * LANES + EXTRA] * 2 + [half * LANES] * 2
    send_far, keep_far, send_near, keep_near = pl.pallas_call(
        functools.partial(moments_kernel, zs),
        out_shape=[jax.ShapeDtypeStruct((n, LANES), F32) for n in shapes],
        scratch_shapes=[pltpu.VMEM((paths, points), F32), pltpu.VMEM((2 * LANES, LANES), F32)],
        compiler_params=limit,
        name="moments",
    )(lows, *others, held_noise, times_row)

    swap = [(i, i ^ 1) for i in range(groups)]
    far = keep_far + lax.ppermute(send_far, "path", swap)
    near = keep_near + lax.ppermute(send_near, "path", swap)
    scale = pl.pallas_call(
        functools.partial(scale_kernel, inner_total),
        out_shape=jax.ShapeDtypeStruct((LANES, LANES), F32),
        compiler_params=limit,
        name="scale",
    )(outer_noise, start_row, vol_row, times_row)
    extra = far[half * LANES :]
    arrived = []
    for step in range(zs - 1):
        s = zs - 1 - step
        held, at = (far, step) if s >= half else (near, step - half)
        message = jnp.concatenate([held[at * LANES : (at + 1) * LANES], extra], axis=0)
        arrived.append(lax.ppermute(message, "path", [(i, i ^ (2 * s)) for i in range(groups)]))
    own = near[(half - 1) * LANES :]

    value, grad, point, point_grad = pl.pallas_call(
        functools.partial(final_kernel, inner_total, len(arrived)),
        out_shape=[
            jax.ShapeDtypeStruct((1, 1), F32),
            jax.ShapeDtypeStruct((1, rows), F32),
            jax.ShapeDtypeStruct((1, points // groups), F32),
            jax.ShapeDtypeStruct((points // groups, rows), F32),
        ],
        compiler_params=limit,
        name="final",
    )(own, extra, scale, outer_noise, start_row, vol_row, times_row, *arrived)
    return value.reshape(1), grad.reshape(rows), point.reshape(points // groups), jnp.transpose(point_grad)


def per_device(inner_noise, outer_noise, start, vol, times):
    rows, points = outer_noise.shape
    groups, dims = lax.axis_size("path"), lax.axis_size("dim")
    fits = (
        2 * points == LANES * groups
        and LANES < rows <= 2 * LANES
        and is_power(groups)
        and groups >= 4
        and dims == 4
        and points // LANES + 2 <= EXTRA
    )
    return (paired if fits else general)(inner_noise, outer_noise, start, vol, times)


def solution(mesh):
    in_specs = (P("path", "dim", None), P("dim", None), P("dim"), P("dim"), P())
    out_specs = (P(), P("dim"), P("path"), P("dim", "path"))
    return jax.shard_map(
        per_device, mesh=mesh, in_specs=in_specs, out_specs=out_specs, check_vma=False
    )
```

```python
import functools

import jax
import jax.numpy as jnp
from jax import lax
from jax.experimental import pallas as pl
from jax.experimental.pallas import tpu as pltpu
from jax.sharding import PartitionSpec as P

drift = 0.02
delta = 2.0 / 3.0
rate_free = 0.02
gamma_high = 0.2
gamma_low = 0.02
value_high = 0.4
value_low = 0.7

LANES = 128
HALF = LANES // 2
EXTRA = 8
CHUNKS = 4
STEP = 8
F32 = jnp.float32


def driver_of(value):
    slope = jnp.clip((value - value_high) / (value_low - value_high), 0.0, 1.0)
    quota = gamma_high + (gamma_low - gamma_high) * slope
    return -(1.0 - delta) * quota * value - rate_free * value


def is_power(n):
    return n > 0 and n & (n - 1) == 0


def general(inner_noise, outer_noise, start, vol, times):
    paths_here = inner_noise.shape[0]
    points = times.shape[0]
    groups = lax.axis_size("path")
    inner_total = paths_here * groups
    owned = points // groups
    tau = 1.0 - times
    outer = outer_noise.astype(F32)
    mean_rate = (drift - 0.5 * vol * vol)[:, None]
    outer_state = start[:, None] * jnp.exp(
        mean_rate * times[None, :] + vol[:, None] * jnp.sqrt(times)[None, :] * outer
    )
    shock = inner_noise.astype(F32)
    level = outer_state[None] * jnp.exp(
        (mean_rate * tau[None, :])[None] + (vol[:, None] * jnp.sqrt(tau)[None, :])[None] * shock
    )
    payoff = lax.pmin(jnp.min(level, axis=1), "dim")
    totals = jnp.sum(payoff, axis=0)
    moments = jnp.sum(payoff[:, None, :] * shock, axis=0)
    start_index = lax.axis_index("path") * owned
    totals, moments = lax.psum((totals, moments), "path")
    point_value = totals / inner_total
    point_grad_all = moments / (inner_total * vol[:, None] * outer_state * jnp.sqrt(tau)[None, :])
    driver = driver_of(point_value)
    root_value = jnp.sum(totals) / (points * inner_total) + jnp.sum(driver) / points
    terminal = jnp.sum(
        jnp.sqrt(times)[None, :] * outer * totals[None, :] + jnp.sqrt(tau)[None, :] * moments,
        axis=1,
    )
    integral = jnp.sum(driver[None, :] * outer / jnp.sqrt(times)[None, :], axis=1)
    root_grad = terminal / (points * inner_total * vol * start) + integral / (points * vol * start)
    own_value = lax.dynamic_slice_in_dim(point_value, start_index, owned, 0)
    own_grad = lax.dynamic_slice_in_dim(point_grad_all, start_index, owned, 1)
    return (jnp.reshape(root_value, (1,)), root_grad, own_value, own_grad)


def row_tiles(rows):
    return [(r, min(16, rows - r)) for r in range(0, rows, 16)]


def as_columns(row, rows):
    full = -(-rows // LANES) * LANES
    row = jnp.concatenate([row, jnp.ones((1, full - rows), F32)], axis=1)
    return jnp.transpose(jnp.broadcast_to(row, (8, full)))[:, 0:1]


def swap_halves(block):
    return pltpu.roll(block, HALF, 1)


def low_lanes(shape):
    return lax.broadcasted_iota(jnp.int32, shape, 1) < HALF


def pack_low(top, bottom):
    return jnp.where(low_lanes(top.shape), top, swap_halves(bottom))


def pack_high(top, bottom):
    return jnp.where(low_lanes(top.shape), swap_halves(top), bottom)


def minima_kernel(
    noise_hbm, outer_hbm, start_hbm, vol_hbm, times_hbm, out_ref, noise_v,
    outer_ref, start_ref, vol_ref, times_ref, level_v, slope_v, sems,
):
    rows, paths, points = noise_hbm.shape
    cuts = [rows * c // CHUNKS // 16 * 16 for c in range(CHUNKS)] + [rows]
    spans = list(zip(cuts[:-1], cuts[1:]))
    copies = [
        pltpu.make_async_copy(noise_hbm.at[lo:hi], noise_v.at[lo:hi], sems.at[c])
        for c, (lo, hi) in enumerate(spans)
    ]
    small = [
        pltpu.make_async_copy(src, dst, sems.at[CHUNKS + c])
        for c, (src, dst) in enumerate(
            [(vol_hbm, vol_ref), (start_hbm, start_ref), (times_hbm, times_ref), (outer_hbm, outer_ref)]
        )
    ]
    for c in small + copies:
        c.start()
    for c in small[:3]:
        c.wait()
    vol_row = vol_ref[...]
    base = as_columns(jnp.log(start_ref[...]) + (drift - 0.5 * vol_row * vol_row), rows)
    vol = as_columns(vol_row, rows)
    times = times_ref[...]
    root_times = jnp.sqrt(times)
    root_tau = jnp.sqrt(1.0 - times)
    small[3].wait()
    for r, n in row_tiles(rows):
        v = vol[r : r + n]
        level_v[r : r + n, :] = base[r : r + n] + (v * root_times) * outer_ref[r : r + n, :].astype(F32)
        slope_v[r : r + n, :] = v * root_tau

    def level(d):
        shock = noise_v[d].astype(F32)
        return level_v[pl.ds(d, 1), :] + slope_v[pl.ds(d, 1), :] * shock

    low = jnp.full((paths, points), jnp.inf, F32)
    for (lo, hi), c in zip(spans, copies):
        c.wait()
        size = hi - lo
        whole = size // STEP

        def body(t, low, lo=lo):
            for j in range(STEP):
                low = jnp.minimum(low, level(lo + t * STEP + j))
            return low

        low = lax.fori_loop(0, whole, body, low)
        for d in range(lo + whole * STEP, hi):
            low = jnp.minimum(low, level(d))
    out_ref[...] = low


def moments_kernel(zs, l0, l1, l2, l3, noise_ref, times_ref, *rest):
    half = zs // 2
    send_far, keep_far, keep_near = rest[:3]
    send_near = rest[3 : 2 + half]
    pay, term = rest[2 + half :]
    paths, rows, points = noise_ref.shape
    me = lax.axis_index("path")
    z = me // 2
    first = me % 2 == 0
    payoff = jnp.exp(jnp.minimum(jnp.minimum(l0[...], l1[...]), jnp.minimum(l2[...], l3[...])))
    pay[...] = payoff
    totals = jnp.sum(payoff, axis=0, keepdims=True)
    for step in range(zs):
        s = zs - 1 - step
        columns = pl.ds(pl.multiple_of((z ^ s) * LANES, LANES), LANES)
        weights = [pay[k : k + 1, columns] for k in range(paths)]
        root_tau = jnp.sqrt(1.0 - times_ref[0:1, columns])
        if s >= half:
            (same, at), (other, past) = (keep_far, step * LANES), (send_far, step * LANES)
        else:
            near = keep_near if s == 0 else send_near[s - 1]
            (same, at), (other, past) = (near, 0), (near, LANES)

        def tile(r):
            n = min(16, rows - r)
            if n <= 0:
                return jnp.zeros((16, LANES), F32)
            total = weights[0] * noise_ref[0, r : r + n, columns].astype(F32)
            for k in range(1, paths):
                total = total + weights[k] * noise_ref[k, r : r + n, columns].astype(F32)
            if n < 16:
                total = jnp.concatenate([total, jnp.zeros((16 - n, LANES), F32)], axis=0)
            return total

        for r in range(0, LANES, 16):
            top, bottom = tile(r), tile(LANES + r)
            low, high = pack_low(top, bottom), pack_high(top, bottom)
            same[at + r : at + r + 16, :] = jnp.where(first, low, high)
            other[past + r : past + r + 16, :] = jnp.where(first, high, low)
            for to, part in ((r, top), (LANES + r, bottom)):
                if step == 0:
                    term[to : to + 16, :] = root_tau * part
                else:
                    term[to : to + 16, :] += root_tau * part
    extras = [totals[:, c : c + LANES] for c in range(0, points, LANES)]
    for r in (0, LANES):
        extras.append(jnp.sum(jnp.transpose(term[r : r + LANES, :]), axis=0, keepdims=True))
    extras.append(jnp.zeros((EXTRA - len(extras), LANES), F32))
    extras = jnp.concatenate(extras, axis=0)
    for ref in (send_far, keep_far, *send_near):
        ref[ref.shape[0] - EXTRA :, :] = extras
    keep_near[2 * LANES :, :] = jnp.zeros((EXTRA, LANES), F32)


def scale_kernel(inner_total, outer_ref, start_ref, vol_ref, times_ref, out_ref):
    rows = outer_ref.shape[0]
    me = lax.axis_index("path")
    z = me // 2
    first = me % 2 == 0
    columns = pl.ds(pl.multiple_of(z * LANES, LANES), LANES)

    def pack(top, bottom):
        return jnp.where(first, pack_low(top, bottom), pack_high(top, bottom))

    vol = as_columns(vol_ref[...], rows)
    start = as_columns(start_ref[...], rows)
    spare = jnp.zeros((2 * LANES - rows, LANES), F32)
    outer = outer_ref[:, columns].astype(F32)
    outer = pack(outer[0:LANES], jnp.concatenate([outer[LANES:rows], spare], axis=0))
    times = times_ref[0:1, columns]
    times = pack(times, times)
    side = low_lanes((LANES, LANES))
    vol = jnp.where(side, vol[0:LANES], vol[LANES:])
    start = jnp.where(side, start[0:LANES], start[LANES:])
    state = start * jnp.exp((drift - 0.5 * vol * vol) * times + vol * jnp.sqrt(times) * outer)
    out_ref[...] = 1.0 / (inner_total * vol * state * jnp.sqrt(1.0 - times))


def final_kernel(
    inner_total, n_parts, near_ref, far_extra_ref, scale_ref, outer_ref, start_ref, vol_ref, times_ref, *rest
):
    parts, (value_ref, grad_ref, point_ref, point_grad_ref) = rest[:n_parts], rest[n_parts:]
    rows, points = outer_ref.shape
    me = lax.axis_index("path")
    first = me % 2 == 0
    moments = near_ref[0:LANES, :]
    extra = far_extra_ref[...] + near_ref[2 * LANES : 2 * LANES + EXTRA, :]
    for part in parts:
        moments = moments + part[0:LANES, :]
        extra = extra + part[LANES : LANES + EXTRA, :]
    grad = moments * scale_ref[...]
    turned = jnp.transpose(grad)
    point_grad_ref[:, 0:LANES] = turned[0:HALF]
    point_grad_ref[:, LANES:rows] = turned[HALF:, 0 : rows - LANES]
    blocks = points // LANES
    totals = jnp.concatenate([extra[c : c + 1, :] for c in range(blocks)], axis=1)
    inner_term = jnp.concatenate([extra[blocks : blocks + 1, :], extra[blocks + 1 : blocks + 2, :]], axis=1)
    values = totals / inner_total
    driver = driver_of(values)
    value_ref[...] = jnp.sum(totals, axis=1, keepdims=True) / (points * inner_total) + (
        jnp.sum(driver, axis=1, keepdims=True) / points
    )
    own = extra[0:1, :]
    for c in range(1, blocks):
        own = jnp.where(me // 2 == c, extra[c : c + 1, :], own)
    own = jnp.where(first, own, swap_halves(own)) / inner_total
    point_ref[...] = own[:, 0:HALF]
    root_times = jnp.sqrt(times_ref[...])
    weight = totals * root_times / inner_total + driver / root_times
    outer_term = lax.dot_general(
        jnp.broadcast_to(weight, (8, points)),
        outer_ref[...].astype(F32),
        (((1,), (1,)), ((), ())),
        precision=lax.Precision.HIGHEST,
        preferred_element_type=F32,
    )[0:1, :]
    grad_ref[...] = (inner_term[:, 0:rows] / inner_total + outer_term) / (
        points * vol_ref[...] * start_ref[...]
    )


def paired(inner_noise, outer_noise, start, vol, times):
    paths, rows, points = inner_noise.shape
    groups, dims = lax.axis_size("path"), lax.axis_size("dim")
    inner_total = paths * groups
    zs = groups // 2
    half = zs // 2
    start_row, vol_row, times_row = start[None, :], vol[None, :], times[None, :]
    limit = pltpu.CompilerParams(vmem_limit_bytes=16 * 1024 * 1024)

    lows, held_noise = pl.pallas_call(
        minima_kernel,
        out_shape=(
            pltpu.VMEM((paths, points), F32),
            pltpu.VMEM((rows, paths, points), inner_noise.dtype),
        ),
        in_specs=[pl.BlockSpec(memory_space=pltpu.HBM)] * 5,
        scratch_shapes=[
            pltpu.VMEM((rows, points), outer_noise.dtype),
            pltpu.VMEM((1, rows), F32),
            pltpu.VMEM((1, rows), F32),
            pltpu.VMEM((1, points), F32),
            pltpu.VMEM((rows, points), F32),
            pltpu.VMEM((rows, points), F32),
            pltpu.SemaphoreType.DMA((CHUNKS + 4,)),
        ],
        compiler_params=limit,
        name="minima",
    )(*[
        pltpu.with_memory_space_constraint(x, pltpu.HBM)
        for x in (jnp.transpose(inner_noise, (1, 0, 2)), outer_noise, start_row, vol_row, times_row)
    ])
    held_noise = jnp.transpose(held_noise, (1, 0, 2))

    others = [
        lax.ppermute(lows, "dim", [(i, i ^ s) for i in range(dims)]) for s in range(1, dims)
    ]
    send_far, keep_far, keep_near, *send_near = pl.pallas_call(
        functools.partial(moments_kernel, zs),
        out_shape=[jax.ShapeDtypeStruct((half * LANES + EXTRA, LANES), F32)] * 2
        + [jax.ShapeDtypeStruct((2 * LANES + EXTRA, LANES), F32)] * half,
        scratch_shapes=[pltpu.VMEM((paths, points), F32), pltpu.VMEM((2 * LANES, LANES), F32)],
        compiler_params=limit,
        name="moments",
    )(lows, *others, held_noise, times_row)

    def along_z(message, s):
        return lax.ppermute(message, "path", [(i, i ^ (2 * s)) for i in range(groups)])

    def along_y(message):
        return lax.ppermute(message, "path", [(i, i ^ 1) for i in range(groups)])

    far = keep_far + along_y(send_far)
    near = keep_near
    for s in range(1, half):
        near = near + along_z(send_near[s - 1], s)
    scale = pl.pallas_call(
        functools.partial(scale_kernel, inner_total),
        out_shape=jax.ShapeDtypeStruct((LANES, LANES), F32),
        compiler_params=limit,
        name="scale",
    )(outer_noise, start_row, vol_row, times_row)
    far_extra = far[half * LANES :]
    arrived = []
    for step in range(half):
        block = far[step * LANES : (step + 1) * LANES]
        arrived.append(along_z(jnp.concatenate([block, far_extra], axis=0), zs - 1 - step))
    arrived.append(along_y(near[LANES:]))

    value, grad, point, point_grad = pl.pallas_call(
        functools.partial(final_kernel, inner_total, len(arrived)),
        out_shape=[
            jax.ShapeDtypeStruct((1, 1), F32),
            jax.ShapeDtypeStruct((1, rows), F32),
            jax.ShapeDtypeStruct((1, points // groups), F32),
            jax.ShapeDtypeStruct((points // groups, rows), F32),
        ],
        compiler_params=limit,
        name="final",
    )(near, far_extra, scale, outer_noise, start_row, vol_row, times_row, *arrived)
    return value.reshape(1), grad.reshape(rows), point.reshape(points // groups), jnp.transpose(point_grad)


def per_device(inner_noise, outer_noise, start, vol, times):
    rows, points = outer_noise.shape
    groups, dims = lax.axis_size("path"), lax.axis_size("dim")
    fits = (
        2 * points == LANES * groups
        and LANES < rows <= 2 * LANES
        and is_power(groups)
        and groups >= 4
        and dims == 4
        and points // LANES + 2 <= EXTRA
    )
    return (paired if fits else general)(inner_noise, outer_noise, start, vol, times)


def solution(mesh):
    in_specs = (P("path", "dim", None), P("dim", None), P("dim"), P("dim"), P())
    out_specs = (P(), P("dim"), P("path"), P("dim", "path"))
    return jax.shard_map(
        per_device, mesh=mesh, in_specs=in_specs, out_specs=out_specs, check_vma=False
    )
```

```python
import functools

import jax
import jax.numpy as jnp
from jax import lax
from jax.experimental import pallas as pl
from jax.experimental.pallas import tpu as pltpu
from jax.sharding import PartitionSpec as P

drift = 0.02
delta = 2.0 / 3.0
rate_free = 0.02
gamma_high = 0.2
gamma_low = 0.02
value_high = 0.4
value_low = 0.7

LANES = 128
HALF = LANES // 2
EXTRA = 8
CHUNKS = 4
STEP = 8
F32 = jnp.float32


def driver_of(value):
    slope = jnp.clip((value - value_high) / (value_low - value_high), 0.0, 1.0)
    quota = gamma_high + (gamma_low - gamma_high) * slope
    return -(1.0 - delta) * quota * value - rate_free * value


def is_power(n):
    return n > 0 and n & (n - 1) == 0


def general(inner_noise, outer_noise, start, vol, times):
    paths_here = inner_noise.shape[0]
    points = times.shape[0]
    groups = lax.axis_size("path")
    inner_total = paths_here * groups
    owned = points // groups
    tau = 1.0 - times
    outer = outer_noise.astype(F32)
    mean_rate = (drift - 0.5 * vol * vol)[:, None]
    outer_state = start[:, None] * jnp.exp(
        mean_rate * times[None, :] + vol[:, None] * jnp.sqrt(times)[None, :] * outer
    )
    shock = inner_noise.astype(F32)
    level = outer_state[None] * jnp.exp(
        (mean_rate * tau[None, :])[None] + (vol[:, None] * jnp.sqrt(tau)[None, :])[None] * shock
    )
    payoff = lax.pmin(jnp.min(level, axis=1), "dim")
    totals = jnp.sum(payoff, axis=0)
    moments = jnp.sum(payoff[:, None, :] * shock, axis=0)
    start_index = lax.axis_index("path") * owned
    totals, moments = lax.psum((totals, moments), "path")
    point_value = totals / inner_total
    point_grad_all = moments / (inner_total * vol[:, None] * outer_state * jnp.sqrt(tau)[None, :])
    driver = driver_of(point_value)
    root_value = jnp.sum(totals) / (points * inner_total) + jnp.sum(driver) / points
    terminal = jnp.sum(
        jnp.sqrt(times)[None, :] * outer * totals[None, :] + jnp.sqrt(tau)[None, :] * moments,
        axis=1,
    )
    integral = jnp.sum(driver[None, :] * outer / jnp.sqrt(times)[None, :], axis=1)
    root_grad = terminal / (points * inner_total * vol * start) + integral / (points * vol * start)
    own_value = lax.dynamic_slice_in_dim(point_value, start_index, owned, 0)
    own_grad = lax.dynamic_slice_in_dim(point_grad_all, start_index, owned, 1)
    return (jnp.reshape(root_value, (1,)), root_grad, own_value, own_grad)


def row_tiles(rows):
    return [(r, min(16, rows - r)) for r in range(0, rows, 16)]


def as_columns(row, rows):
    full = -(-rows // LANES) * LANES
    row = jnp.concatenate([row, jnp.ones((1, full - rows), F32)], axis=1)
    return jnp.transpose(jnp.broadcast_to(row, (8, full)))[:, 0:1]


def swap_halves(block):
    return pltpu.roll(block, HALF, 1)


def low_lanes(shape):
    return lax.broadcasted_iota(jnp.int32, shape, 1) < HALF


def pack_low(top, bottom):
    return jnp.where(low_lanes(top.shape), top, swap_halves(bottom))


def pack_high(top, bottom):
    return jnp.where(low_lanes(top.shape), swap_halves(top), bottom)


def minima_kernel(
    noise_hbm, outer_hbm, start_hbm, vol_hbm, times_hbm, out_ref, noise_v,
    outer_ref, start_ref, vol_ref, times_ref, level_v, slope_v, sems,
):
    rows, paths, points = noise_hbm.shape
    cuts = [rows * c // CHUNKS // 16 * 16 for c in range(CHUNKS)] + [rows]
    spans = list(zip(cuts[:-1], cuts[1:]))
    copies = [
        pltpu.make_async_copy(noise_hbm.at[lo:hi], noise_v.at[lo:hi], sems.at[c])
        for c, (lo, hi) in enumerate(spans)
    ]
    small = [
        pltpu.make_async_copy(src, dst, sems.at[CHUNKS + c])
        for c, (src, dst) in enumerate(
            [(vol_hbm, vol_ref), (start_hbm, start_ref), (times_hbm, times_ref), (outer_hbm, outer_ref)]
        )
    ]
    for c in small + copies:
        c.start()
    for c in small[:3]:
        c.wait()
    vol_row = vol_ref[...]
    base = as_columns(jnp.log(start_ref[...]) + (drift - 0.5 * vol_row * vol_row), rows)
    vol = as_columns(vol_row, rows)
    times = times_ref[...]
    root_times = jnp.sqrt(times)
    root_tau = jnp.sqrt(1.0 - times)
    small[3].wait()
    for r, n in row_tiles(rows):
        v = vol[r : r + n]
        level_v[r : r + n, :] = base[r : r + n] + (v * root_times) * outer_ref[r : r + n, :].astype(F32)
        slope_v[r : r + n, :] = v * root_tau

    def level(d):
        shock = noise_v[d].astype(F32)
        return level_v[pl.ds(d, 1), :] + slope_v[pl.ds(d, 1), :] * shock

    low = jnp.full((paths, points), jnp.inf, F32)
    for (lo, hi), c in zip(spans, copies):
        c.wait()
        size = hi - lo
        whole = size // STEP

        def body(t, low, lo=lo):
            for j in range(STEP):
                low = jnp.minimum(low, level(lo + t * STEP + j))
            return low

        low = lax.fori_loop(0, whole, body, low)
        for d in range(lo + whole * STEP, hi):
            low = jnp.minimum(low, level(d))
    out_ref[...] = low


def moments_kernel(zs, far, lows_ref, last_ref, noise_ref, times_ref, *rest):
    near = [s for s in range(1, zs) if s not in far]
    send_far, keep_far, keep_near = rest[:3]
    send_near = rest[3 : 3 + len(near)]
    pay, term = rest[3 + len(near) :]
    paths, rows, points = noise_ref.shape
    me = lax.axis_index("path")
    z = me // 2
    first = me % 2 == 0
    payoff = jnp.exp(jnp.minimum(lows_ref[...], last_ref[...]))
    pay[...] = payoff
    totals = jnp.sum(payoff, axis=0, keepdims=True)
    for step in range(zs):
        s = zs - 1 - step
        columns = pl.ds(pl.multiple_of((z ^ s) * LANES, LANES), LANES)
        weights = [pay[k : k + 1, columns] for k in range(paths)]
        root_tau = jnp.sqrt(1.0 - times_ref[0:1, columns])
        if s in far:
            at = past = far.index(s) * LANES
            same, other = keep_far, send_far
        else:
            at, past = 0, LANES
            same = other = keep_near if s == 0 else send_near[near.index(s)]

        def tile(r):
            n = min(16, rows - r)
            if n <= 0:
                return jnp.zeros((16, LANES), F32)
            total = weights[0] * noise_ref[0, r : r + n, columns].astype(F32)
            for k in range(1, paths):
                total = total + weights[k] * noise_ref[k, r : r + n, columns].astype(F32)
            if n < 16:
                total = jnp.concatenate([total, jnp.zeros((16 - n, LANES), F32)], axis=0)
            return total

        for r in range(0, LANES, 16):
            top, bottom = tile(r), tile(LANES + r)
            low, high = pack_low(top, bottom), pack_high(top, bottom)
            same[at + r : at + r + 16, :] = jnp.where(first, low, high)
            other[past + r : past + r + 16, :] = jnp.where(first, high, low)
            for to, part in ((r, top), (LANES + r, bottom)):
                if step == 0:
                    term[to : to + 16, :] = root_tau * part
                else:
                    term[to : to + 16, :] += root_tau * part
    extras = [totals[:, c : c + LANES] for c in range(0, points, LANES)]
    for r in (0, LANES):
        extras.append(jnp.sum(jnp.transpose(term[r : r + LANES, :]), axis=0, keepdims=True))
    extras.append(jnp.zeros((EXTRA - len(extras), LANES), F32))
    extras = jnp.concatenate(extras, axis=0)
    for ref in (send_far, keep_far, *send_near):
        ref[ref.shape[0] - EXTRA :, :] = extras
    keep_near[2 * LANES :, :] = jnp.zeros((EXTRA, LANES), F32)


def scale_kernel(inner_total, outer_ref, start_ref, vol_ref, times_ref, out_ref):
    rows = outer_ref.shape[0]
    me = lax.axis_index("path")
    z = me // 2
    first = me % 2 == 0
    columns = pl.ds(pl.multiple_of(z * LANES, LANES), LANES)

    def pack(top, bottom):
        return jnp.where(first, pack_low(top, bottom), pack_high(top, bottom))

    vol = as_columns(vol_ref[...], rows)
    start = as_columns(start_ref[...], rows)
    spare = jnp.zeros((2 * LANES - rows, LANES), F32)
    outer = outer_ref[:, columns].astype(F32)
    outer = pack(outer[0:LANES], jnp.concatenate([outer[LANES:rows], spare], axis=0))
    times = times_ref[0:1, columns]
    times = pack(times, times)
    side = low_lanes((LANES, LANES))
    vol = jnp.where(side, vol[0:LANES], vol[LANES:])
    start = jnp.where(side, start[0:LANES], start[LANES:])
    state = start * jnp.exp((drift - 0.5 * vol * vol) * times + vol * jnp.sqrt(times) * outer)
    out_ref[...] = 1.0 / (inner_total * vol * state * jnp.sqrt(1.0 - times))


def final_kernel(
    inner_total, n_parts, near_ref, far_extra_ref, scale_ref, outer_ref, start_ref, vol_ref, times_ref, *rest
):
    parts, (value_ref, grad_ref, point_ref, point_grad_ref) = rest[:n_parts], rest[n_parts:]
    rows, points = outer_ref.shape
    me = lax.axis_index("path")
    first = me % 2 == 0
    moments = near_ref[0:LANES, :]
    extra = far_extra_ref[...] + near_ref[2 * LANES : 2 * LANES + EXTRA, :]
    for part in parts:
        moments = moments + part[0:LANES, :]
        extra = extra + part[LANES : LANES + EXTRA, :]
    grad = moments * scale_ref[...]
    turned = jnp.transpose(grad)
    point_grad_ref[:, 0:LANES] = turned[0:HALF]
    point_grad_ref[:, LANES:rows] = turned[HALF:, 0 : rows - LANES]
    blocks = points // LANES
    totals = jnp.concatenate([extra[c : c + 1, :] for c in range(blocks)], axis=1)
    inner_term = jnp.concatenate([extra[blocks : blocks + 1, :], extra[blocks + 1 : blocks + 2, :]], axis=1)
    values = totals / inner_total
    driver = driver_of(values)
    value_ref[...] = jnp.sum(totals, axis=1, keepdims=True) / (points * inner_total) + (
        jnp.sum(driver, axis=1, keepdims=True) / points
    )
    own = extra[0:1, :]
    for c in range(1, blocks):
        own = jnp.where(me // 2 == c, extra[c : c + 1, :], own)
    own = jnp.where(first, own, swap_halves(own)) / inner_total
    point_ref[...] = own[:, 0:HALF]
    root_times = jnp.sqrt(times_ref[...])
    weight = totals * root_times / inner_total + driver / root_times
    outer_term = lax.dot_general(
        jnp.broadcast_to(weight, (8, points)),
        outer_ref[...].astype(F32),
        (((1,), (1,)), ((), ())),
        precision=lax.Precision.HIGHEST,
        preferred_element_type=F32,
    )[0:1, :]
    grad_ref[...] = (inner_term[:, 0:rows] / inner_total + outer_term) / (
        points * vol_ref[...] * start_ref[...]
    )


def paired(inner_noise, outer_noise, start, vol, times):
    paths, rows, points = inner_noise.shape
    groups, dims = lax.axis_size("path"), lax.axis_size("dim")
    inner_total = paths * groups
    zs = groups // 2
    half = zs // 2
    start_row, vol_row, times_row = start[None, :], vol[None, :], times[None, :]
    limit = pltpu.CompilerParams(vmem_limit_bytes=16 * 1024 * 1024)

    lows, held_noise = pl.pallas_call(
        minima_kernel,
        out_shape=(
            pltpu.VMEM((paths, points), F32),
            pltpu.VMEM((rows, paths, points), inner_noise.dtype),
        ),
        in_specs=[pl.BlockSpec(memory_space=pltpu.HBM)] * 5,
        scratch_shapes=[
            pltpu.VMEM((rows, points), outer_noise.dtype),
            pltpu.VMEM((1, rows), F32),
            pltpu.VMEM((1, rows), F32),
            pltpu.VMEM((1, points), F32),
            pltpu.VMEM((rows, points), F32),
            pltpu.VMEM((rows, points), F32),
            pltpu.SemaphoreType.DMA((CHUNKS + 4,)),
        ],
        compiler_params=limit,
        name="minima",
    )(*[
        pltpu.with_memory_space_constraint(x, pltpu.HBM)
        for x in (jnp.transpose(inner_noise, (1, 0, 2)), outer_noise, start_row, vol_row, times_row)
    ])
    held_noise = jnp.transpose(held_noise, (1, 0, 2))

    last = None
    for bit in [1 << n for n in range(dims.bit_length() - 1)]:
        if last is not None:
            lows = jnp.minimum(lows, last)
        last = lax.ppermute(lows, "dim", [(i, i ^ bit) for i in range(dims)])

    far = tuple(range(half, zs))
    near = [s for s in range(1, zs) if s not in far]
    send_far, keep_far, keep_near, *send_near = pl.pallas_call(
        functools.partial(moments_kernel, zs, far),
        out_shape=[jax.ShapeDtypeStruct((len(far) * LANES + EXTRA, LANES), F32)] * 2
        + [jax.ShapeDtypeStruct((2 * LANES + EXTRA, LANES), F32)] * (1 + len(near)),
        scratch_shapes=[pltpu.VMEM((paths, points), F32), pltpu.VMEM((2 * LANES, LANES), F32)],
        compiler_params=limit,
        name="moments",
    )(lows, last, held_noise, times_row)

    def along_z(message, s):
        return lax.ppermute(message, "path", [(i, i ^ (2 * s)) for i in range(groups)])

    def along_y(message):
        return lax.ppermute(message, "path", [(i, i ^ 1) for i in range(groups)])

    far_sum = keep_far + along_y(send_far)
    near_sum = keep_near
    for s, send in zip(near, send_near):
        near_sum = near_sum + along_z(send, s)
    scale = pl.pallas_call(
        functools.partial(scale_kernel, inner_total),
        out_shape=jax.ShapeDtypeStruct((LANES, LANES), F32),
        compiler_params=limit,
        name="scale",
    )(outer_noise, start_row, vol_row, times_row)
    far_extra = far_sum[len(far) * LANES :]
    arrived = []
    for n, s in enumerate(far):
        message = jnp.concatenate([far_sum[n * LANES : (n + 1) * LANES], far_extra], axis=0)
        arrived.append(along_z(message, s))
    arrived.append(along_y(near_sum[LANES:]))

    value, grad, point, point_grad = pl.pallas_call(
        functools.partial(final_kernel, inner_total, len(arrived)),
        out_shape=[
            jax.ShapeDtypeStruct((1, 1), F32),
            jax.ShapeDtypeStruct((1, rows), F32),
            jax.ShapeDtypeStruct((1, points // groups), F32),
            jax.ShapeDtypeStruct((points // groups, rows), F32),
        ],
        compiler_params=limit,
        name="final",
    )(near_sum, far_extra, scale, outer_noise, start_row, vol_row, times_row, *arrived)
    return value.reshape(1), grad.reshape(rows), point.reshape(points // groups), jnp.transpose(point_grad)


def per_device(inner_noise, outer_noise, start, vol, times):
    rows, points = outer_noise.shape
    groups, dims = lax.axis_size("path"), lax.axis_size("dim")
    fits = (
        2 * points == LANES * groups
        and LANES < rows <= 2 * LANES
        and is_power(groups)
        and groups >= 4
        and is_power(dims)
        and dims > 1
        and points // LANES + 2 <= EXTRA
    )
    return (paired if fits else general)(inner_noise, outer_noise, start, vol, times)


def solution(mesh):
    in_specs = (P("path", "dim", None), P("dim", None), P("dim"), P("dim"), P())
    out_specs = (P(), P("dim"), P("path"), P("dim", "path"))
    return jax.shard_map(
        per_device, mesh=mesh, in_specs=in_specs, out_specs=out_specs, check_vma=False
    )
```

```python
import functools

import jax
import jax.numpy as jnp
from jax import lax
from jax.experimental import pallas as pl
from jax.experimental.pallas import tpu as pltpu
from jax.sharding import PartitionSpec as P

drift = 0.02
delta = 2.0 / 3.0
rate_free = 0.02
gamma_high = 0.2
gamma_low = 0.02
value_high = 0.4
value_low = 0.7

LANES = 128
HALF = LANES // 2
EXTRA = 8
CHUNKS = 4
STEP = 16
F32 = jnp.float32


def driver_of(value):
    slope = jnp.clip((value - value_high) / (value_low - value_high), 0.0, 1.0)
    quota = gamma_high + (gamma_low - gamma_high) * slope
    return -(1.0 - delta) * quota * value - rate_free * value


def is_power(n):
    return n > 0 and n & (n - 1) == 0


def general(inner_noise, outer_noise, start, vol, times):
    paths_here = inner_noise.shape[0]
    points = times.shape[0]
    groups = lax.axis_size("path")
    inner_total = paths_here * groups
    owned = points // groups
    tau = 1.0 - times
    outer = outer_noise.astype(F32)
    mean_rate = (drift - 0.5 * vol * vol)[:, None]
    outer_state = start[:, None] * jnp.exp(
        mean_rate * times[None, :] + vol[:, None] * jnp.sqrt(times)[None, :] * outer
    )
    shock = inner_noise.astype(F32)
    level = outer_state[None] * jnp.exp(
        (mean_rate * tau[None, :])[None] + (vol[:, None] * jnp.sqrt(tau)[None, :])[None] * shock
    )
    payoff = lax.pmin(jnp.min(level, axis=1), "dim")
    totals = jnp.sum(payoff, axis=0)
    moments = jnp.sum(payoff[:, None, :] * shock, axis=0)
    start_index = lax.axis_index("path") * owned
    totals, moments = lax.psum((totals, moments), "path")
    point_value = totals / inner_total
    point_grad_all = moments / (inner_total * vol[:, None] * outer_state * jnp.sqrt(tau)[None, :])
    driver = driver_of(point_value)
    root_value = jnp.sum(totals) / (points * inner_total) + jnp.sum(driver) / points
    terminal = jnp.sum(
        jnp.sqrt(times)[None, :] * outer * totals[None, :] + jnp.sqrt(tau)[None, :] * moments,
        axis=1,
    )
    integral = jnp.sum(driver[None, :] * outer / jnp.sqrt(times)[None, :], axis=1)
    root_grad = terminal / (points * inner_total * vol * start) + integral / (points * vol * start)
    own_value = lax.dynamic_slice_in_dim(point_value, start_index, owned, 0)
    own_grad = lax.dynamic_slice_in_dim(point_grad_all, start_index, owned, 1)
    return (jnp.reshape(root_value, (1,)), root_grad, own_value, own_grad)


def row_tiles(rows):
    return [(r, min(16, rows - r)) for r in range(0, rows, 16)]


def as_columns(row, rows):
    full = -(-rows // LANES) * LANES
    row = jnp.concatenate([row, jnp.ones((1, full - rows), F32)], axis=1)
    return jnp.transpose(jnp.broadcast_to(row, (8, full)))[:, 0:1]


def swap_halves(block):
    return pltpu.roll(block, HALF, 1)


def low_lanes(shape):
    return lax.broadcasted_iota(jnp.int32, shape, 1) < HALF


def pack_low(top, bottom):
    return jnp.where(low_lanes(top.shape), top, swap_halves(bottom))


def pack_high(top, bottom):
    return jnp.where(low_lanes(top.shape), swap_halves(top), bottom)


def minima_kernel(
    noise_hbm, outer_hbm, start_hbm, vol_hbm, times_hbm, out_ref, noise_v,
    outer_ref, start_ref, vol_ref, times_ref, vol_s, level_v, sems,
):
    rows, paths, points = noise_hbm.shape
    cuts = [rows * c // CHUNKS // 16 * 16 for c in range(CHUNKS)] + [rows]
    spans = list(zip(cuts[:-1], cuts[1:]))
    copies = [
        pltpu.make_async_copy(noise_hbm.at[lo:hi], noise_v.at[lo:hi], sems.at[c])
        for c, (lo, hi) in enumerate(spans)
    ]
    small = [
        pltpu.make_async_copy(src, dst, sems.at[CHUNKS + c])
        for c, (src, dst) in enumerate(
            [
                (vol_hbm, vol_ref),
                (start_hbm, start_ref),
                (times_hbm, times_ref),
                (vol_hbm, vol_s),
                (outer_hbm, outer_ref),
            ]
        )
    ]
    for c in small + copies:
        c.start()
    for c in small[:4]:
        c.wait()
    vol_row = vol_ref[...]
    base = as_columns(jnp.log(start_ref[...]) + (drift - 0.5 * vol_row * vol_row), rows)
    vol = as_columns(vol_row, rows)
    times = times_ref[...]
    root_tau = jnp.sqrt(1.0 - times)
    inverse = 1.0 / root_tau
    ratio = jnp.sqrt(times) * inverse
    small[4].wait()
    for r, n in row_tiles(rows):
        drifted = base[r : r + n] * inverse
        level_v[r : r + n, :] = drifted + (vol[r : r + n] * ratio) * outer_ref[r : r + n, :].astype(F32)

    def level(d):
        return level_v[pl.ds(d, 1), :] + vol_s[0, d] * noise_v[d].astype(F32)

    low = jnp.full((paths, points), jnp.inf, F32)
    for (lo, hi), c in zip(spans, copies):
        c.wait()
        size = hi - lo
        whole = size // STEP

        def body(t, low, lo=lo):
            for j in range(STEP):
                low = jnp.minimum(low, level(lo + t * STEP + j))
            return low

        low = lax.fori_loop(0, whole, body, low)
        for d in range(lo + whole * STEP, hi):
            low = jnp.minimum(low, level(d))
    out_ref[...] = low * root_tau


def split(value):
    parts = []
    for _ in range(3):
        part = value.astype(jnp.bfloat16)
        value = value - part.astype(F32)
        parts.append(part)
    return parts


def parts_kernel(zs, noise_ref, out_ref):
    paths, rows, points = noise_ref.shape
    me = lax.axis_index("path")
    z, y = me // 2, me % 2
    for s in range(zs):
        columns = pl.ds(pl.multiple_of((z ^ s) * LANES, LANES), LANES)

        def tile(k, r):
            n = min(16, rows - r)
            if n <= 0:
                return jnp.zeros((16, LANES), F32)
            part = noise_ref[k, r : r + n, columns].astype(F32)
            if n < 16:
                part = jnp.concatenate([part, jnp.zeros((16 - n, LANES), F32)], axis=0)
            return part

        for k in range(paths):
            for r in range(0, LANES, 16):
                top, bottom = tile(k, r), tile(k, LANES + r)
                out_ref[k, 2 * s + y, r : r + 16, :] = pack_low(top, bottom)
                out_ref[k, 2 * s + 1 - y, r : r + 16, :] = pack_high(top, bottom)


def moments_kernel(zs, far, lows_ref, last_ref, parts_ref, times_ref, *rest):
    near = [s for s in range(1, zs) if s not in far]
    send_far, keep_far, keep_near = rest[:3]
    send_near = rest[3 : 3 + len(near)]
    pay, term = rest[3 + len(near) :]
    paths, points = lows_ref.shape
    me = lax.axis_index("path")
    z = me // 2
    first = me % 2 == 0
    payoff = jnp.exp(jnp.minimum(lows_ref[...], last_ref[...]))
    pay[...] = payoff
    totals = jnp.sum(payoff, axis=0, keepdims=True)
    for s in range(zs):
        columns = pl.ds(pl.multiple_of((z ^ s) * LANES, LANES), LANES)
        both = jnp.concatenate([pay[:, columns], jnp.sqrt(1.0 - times_ref[0:1, columns])], axis=0)
        low, high = pack_low(both, both), pack_high(both, both)
        if s in far:
            at = past = far.index(s) * LANES
            same, other = keep_far, send_far
        else:
            at, past = 0, LANES
            same = other = keep_near if s == 0 else send_near[near.index(s)]
        for half, (ref, place) in enumerate(((same, at), (other, past))):
            rows = jnp.where(first, low, high) if half == 0 else jnp.where(first, high, low)
            weights = [jnp.broadcast_to(rows[k : k + 1], (8, LANES)) for k in range(paths + 1)]
            for r in range(0, LANES, 8):
                total = weights[0] * parts_ref[0, 2 * s + half, r : r + 8, :]
                for k in range(1, paths):
                    total = total + weights[k] * parts_ref[k, 2 * s + half, r : r + 8, :]
                ref[place + r : place + r + 8, :] = total
                if s == 0 and half == 0:
                    term[r : r + 8, :] = weights[paths] * total
                else:
                    term[r : r + 8, :] += weights[paths] * total
    extras = [totals[:, c : c + LANES] for c in range(0, points, LANES)]
    side = lax.broadcasted_iota(jnp.int32, (16, LANES), 1) // HALF
    picks = (lax.broadcasted_iota(jnp.int32, (16, LANES), 0) == side).astype(F32).astype(jnp.bfloat16)
    sums = sum(
        lax.dot_general(picks, part, (((1,), (1,)), ((), ())), preferred_element_type=F32)
        for part in split(term[...])
    )
    extras.append(sums[0 : EXTRA - len(extras), :])
    extras = jnp.concatenate(extras, axis=0)
    for ref in (send_far, keep_far, *send_near):
        ref[ref.shape[0] - EXTRA :, :] = extras
    keep_near[2 * LANES :, :] = jnp.zeros((EXTRA, LANES), F32)


def scale_kernel(inner_total, outer_ref, start_ref, vol_ref, times_ref, out_ref):
    rows = outer_ref.shape[0]
    me = lax.axis_index("path")
    z = me // 2
    first = me % 2 == 0
    columns = pl.ds(pl.multiple_of(z * LANES, LANES), LANES)

    def pack(top, bottom):
        return jnp.where(first, pack_low(top, bottom), pack_high(top, bottom))

    vol = as_columns(vol_ref[...], rows)
    start = as_columns(start_ref[...], rows)
    spare = jnp.zeros((2 * LANES - rows, LANES), F32)
    outer = outer_ref[:, columns].astype(F32)
    outer = pack(outer[0:LANES], jnp.concatenate([outer[LANES:rows], spare], axis=0))
    times = times_ref[0:1, columns]
    times = pack(times, times)
    side = low_lanes((LANES, LANES))
    vol = jnp.where(side, vol[0:LANES], vol[LANES:])
    start = jnp.where(side, start[0:LANES], start[LANES:])
    state = start * jnp.exp((drift - 0.5 * vol * vol) * times + vol * jnp.sqrt(times) * outer)
    out_ref[...] = 1.0 / (inner_total * vol * state * jnp.sqrt(1.0 - times))


def final_kernel(
    inner_total, n_parts, near_ref, far_extra_ref, scale_ref, outer_ref, start_ref, vol_ref, times_ref, *rest
):
    parts, (value_ref, grad_ref, point_ref, point_grad_ref) = rest[:n_parts], rest[n_parts:]
    rows, points = outer_ref.shape
    me = lax.axis_index("path")
    first = me % 2 == 0
    moments = near_ref[0:LANES, :]
    extra = far_extra_ref[...] + near_ref[2 * LANES : 2 * LANES + EXTRA, :]
    for part in parts:
        moments = moments + part[0:LANES, :]
        extra = extra + part[LANES : LANES + EXTRA, :]
    grad = moments * scale_ref[...]
    turned = jnp.transpose(grad)
    point_grad_ref[:, 0:LANES] = turned[0:HALF]
    point_grad_ref[:, LANES:rows] = turned[HALF:, 0 : rows - LANES]
    blocks = points // LANES
    totals = jnp.concatenate([extra[c : c + 1, :] for c in range(blocks)], axis=1)
    inner_term = jnp.concatenate([extra[blocks : blocks + 1, :], extra[blocks + 1 : blocks + 2, :]], axis=1)
    values = totals / inner_total
    driver = driver_of(values)
    value_ref[...] = jnp.sum(totals, axis=1, keepdims=True) / (points * inner_total) + (
        jnp.sum(driver, axis=1, keepdims=True) / points
    )
    own = extra[0:1, :]
    for c in range(1, blocks):
        own = jnp.where(me // 2 == c, extra[c : c + 1, :], own)
    own = jnp.where(first, own, swap_halves(own)) / inner_total
    point_ref[...] = own[:, 0:HALF]
    root_times = jnp.sqrt(times_ref[...])
    weight = totals * root_times / inner_total + driver / root_times
    parts_of = [part.astype(F32) for part in split(weight)]
    weights = jnp.concatenate(parts_of + [jnp.zeros((13, points), F32)], axis=0).astype(jnp.bfloat16)
    outer_term = jnp.sum(
        lax.dot_general(
            weights, outer_ref[...], (((1,), (1,)), ((), ())), preferred_element_type=F32
        ),
        axis=0,
        keepdims=True,
    )
    grad_ref[...] = (inner_term[:, 0:rows] / inner_total + outer_term) / (
        points * vol_ref[...] * start_ref[...]
    )


def paired(inner_noise, outer_noise, start, vol, times):
    paths, rows, points = inner_noise.shape
    groups, dims = lax.axis_size("path"), lax.axis_size("dim")
    inner_total = paths * groups
    zs = groups // 2
    half = zs // 2
    start_row, vol_row, times_row = start[None, :], vol[None, :], times[None, :]
    limit = pltpu.CompilerParams(vmem_limit_bytes=16 * 1024 * 1024)

    lows, held_noise = pl.pallas_call(
        minima_kernel,
        out_shape=(
            pltpu.VMEM((paths, points), F32),
            pltpu.VMEM((rows, paths, points), inner_noise.dtype),
        ),
        in_specs=[pl.BlockSpec(memory_space=pltpu.HBM)] * 5,
        scratch_shapes=[
            pltpu.VMEM((rows, points), outer_noise.dtype),
            pltpu.VMEM((1, rows), F32),
            pltpu.VMEM((1, rows), F32),
            pltpu.VMEM((1, points), F32),
            pltpu.SMEM((1, rows), F32),
            pltpu.VMEM((rows, points), F32),
            pltpu.SemaphoreType.DMA((CHUNKS + 5,)),
        ],
        compiler_params=limit,
        name="minima",
    )(*[
        pltpu.with_memory_space_constraint(x, pltpu.HBM)
        for x in (jnp.transpose(inner_noise, (1, 0, 2)), outer_noise, start_row, vol_row, times_row)
    ])
    held_noise = jnp.transpose(held_noise, (1, 0, 2))

    last = None
    for bit in [1 << n for n in range(dims.bit_length() - 1)]:
        if last is not None:
            lows = jnp.minimum(lows, last)
        last = lax.ppermute(lows, "dim", [(i, i ^ bit) for i in range(dims)])

    parts = pl.pallas_call(
        functools.partial(parts_kernel, zs),
        out_shape=pltpu.VMEM((paths, 2 * zs, LANES, LANES), F32),
        compiler_params=limit,
        cost_estimate=pl.CostEstimate(
            flops=paths * rows * points, bytes_accessed=6 * paths * rows * points, transcendentals=0
        ),
        name="parts",
    )(held_noise)

    far = tuple(range(half, zs))
    near = [s for s in range(1, zs) if s not in far]
    send_far, keep_far, keep_near, *send_near = pl.pallas_call(
        functools.partial(moments_kernel, zs, far),
        out_shape=[pltpu.VMEM((len(far) * LANES + EXTRA, LANES), F32)] * 2
        + [pltpu.VMEM((2 * LANES + EXTRA, LANES), F32)] * (1 + len(near)),
        scratch_shapes=[pltpu.VMEM((paths, points), F32), pltpu.VMEM((LANES, LANES), F32)],
        compiler_params=limit,
        name="moments",
    )(lows, last, parts, times_row)

    def along_z(message, s):
        return lax.ppermute(message, "path", [(i, i ^ (2 * s)) for i in range(groups)])

    def along_y(message):
        return lax.ppermute(message, "path", [(i, i ^ 1) for i in range(groups)])

    far_sum = keep_far + along_y(send_far)
    near_sum = keep_near
    for s, send in zip(near, send_near):
        near_sum = near_sum + along_z(send, s)
    scale = pl.pallas_call(
        functools.partial(scale_kernel, inner_total),
        out_shape=pltpu.VMEM((LANES, LANES), F32),
        compiler_params=limit,
        name="scale",
    )(outer_noise, start_row, vol_row, times_row)
    far_extra = far_sum[len(far) * LANES :]
    arrived = []
    for n, s in enumerate(far):
        message = jnp.concatenate([far_sum[n * LANES : (n + 1) * LANES], far_extra], axis=0)
        arrived.append(along_z(message, s))
    arrived.append(along_y(near_sum[LANES:]))

    value, grad, point, point_grad = pl.pallas_call(
        functools.partial(final_kernel, inner_total, len(arrived)),
        out_shape=[
            jax.ShapeDtypeStruct((1, 1), F32),
            jax.ShapeDtypeStruct((1, rows), F32),
            jax.ShapeDtypeStruct((1, points // groups), F32),
            jax.ShapeDtypeStruct((points // groups, rows), F32),
        ],
        compiler_params=limit,
        name="final",
    )(near_sum, far_extra, scale, outer_noise, start_row, vol_row, times_row, *arrived)
    return value.reshape(1), grad.reshape(rows), point.reshape(points // groups), jnp.transpose(point_grad)


def per_device(inner_noise, outer_noise, start, vol, times):
    rows, points = outer_noise.shape
    groups, dims = lax.axis_size("path"), lax.axis_size("dim")
    fits = (
        2 * points == LANES * groups
        and LANES < rows <= 2 * LANES
        and is_power(groups)
        and groups >= 4
        and is_power(dims)
        and dims > 1
        and points // LANES + 2 <= EXTRA
    )
    return (paired if fits else general)(inner_noise, outer_noise, start, vol, times)


def solution(mesh):
    in_specs = (P("path", "dim", None), P("dim", None), P("dim"), P("dim"), P())
    out_specs = (P(), P("dim"), P("path"), P("dim", "path"))
    return jax.shard_map(
        per_device, mesh=mesh, in_specs=in_specs, out_specs=out_specs, check_vma=False
    )
```

```python
import functools

import jax
import jax.numpy as jnp
from jax import lax
from jax.experimental import pallas as pl
from jax.experimental.pallas import tpu as pltpu
from jax.sharding import PartitionSpec as P

drift = 0.02
delta = 2.0 / 3.0
rate_free = 0.02
gamma_high = 0.2
gamma_low = 0.02
value_high = 0.4
value_low = 0.7

LANES = 128
HALF = LANES // 2
EXTRA = 8
CHUNKS = 4
STEP = 16
F32 = jnp.float32


def driver_of(value):
    slope = jnp.clip((value - value_high) / (value_low - value_high), 0.0, 1.0)
    quota = gamma_high + (gamma_low - gamma_high) * slope
    return -(1.0 - delta) * quota * value - rate_free * value


def is_power(n):
    return n > 0 and n & (n - 1) == 0


def general(inner_noise, outer_noise, start, vol, times):
    paths_here = inner_noise.shape[0]
    points = times.shape[0]
    groups = lax.axis_size("path")
    inner_total = paths_here * groups
    owned = points // groups
    tau = 1.0 - times
    outer = outer_noise.astype(F32)
    mean_rate = (drift - 0.5 * vol * vol)[:, None]
    outer_state = start[:, None] * jnp.exp(
        mean_rate * times[None, :] + vol[:, None] * jnp.sqrt(times)[None, :] * outer
    )
    shock = inner_noise.astype(F32)
    level = outer_state[None] * jnp.exp(
        (mean_rate * tau[None, :])[None] + (vol[:, None] * jnp.sqrt(tau)[None, :])[None] * shock
    )
    payoff = lax.pmin(jnp.min(level, axis=1), "dim")
    totals = jnp.sum(payoff, axis=0)
    moments = jnp.sum(payoff[:, None, :] * shock, axis=0)
    start_index = lax.axis_index("path") * owned
    totals, moments = lax.psum((totals, moments), "path")
    point_value = totals / inner_total
    point_grad_all = moments / (inner_total * vol[:, None] * outer_state * jnp.sqrt(tau)[None, :])
    driver = driver_of(point_value)
    root_value = jnp.sum(totals) / (points * inner_total) + jnp.sum(driver) / points
    terminal = jnp.sum(
        jnp.sqrt(times)[None, :] * outer * totals[None, :] + jnp.sqrt(tau)[None, :] * moments,
        axis=1,
    )
    integral = jnp.sum(driver[None, :] * outer / jnp.sqrt(times)[None, :], axis=1)
    root_grad = terminal / (points * inner_total * vol * start) + integral / (points * vol * start)
    own_value = lax.dynamic_slice_in_dim(point_value, start_index, owned, 0)
    own_grad = lax.dynamic_slice_in_dim(point_grad_all, start_index, owned, 1)
    return (jnp.reshape(root_value, (1,)), root_grad, own_value, own_grad)


def row_tiles(rows):
    return [(r, min(16, rows - r)) for r in range(0, rows, 16)]


def as_columns(row, rows):
    full = -(-rows // LANES) * LANES
    row = jnp.concatenate([row, jnp.ones((1, full - rows), F32)], axis=1)
    return jnp.transpose(jnp.broadcast_to(row, (8, full)))[:, 0:1]


def swap_halves(block):
    return pltpu.roll(block, HALF, 1)


def low_lanes(shape):
    return lax.broadcasted_iota(jnp.int32, shape, 1) < HALF


def pack_low(top, bottom):
    return jnp.where(low_lanes(top.shape), top, swap_halves(bottom))


def pack_high(top, bottom):
    return jnp.where(low_lanes(top.shape), swap_halves(top), bottom)


def minima_kernel(
    noise_hbm, outer_hbm, start_hbm, vol_hbm, times_hbm, out_ref, noise_v,
    outer_ref, start_ref, vol_ref, times_ref, vol_s, level_v, sems,
):
    rows, paths, points = noise_hbm.shape
    cuts = [rows * c // CHUNKS // 16 * 16 for c in range(CHUNKS)] + [rows]
    spans = list(zip(cuts[:-1], cuts[1:]))
    copies = [
        pltpu.make_async_copy(noise_hbm.at[lo:hi], noise_v.at[lo:hi], sems.at[c])
        for c, (lo, hi) in enumerate(spans)
    ]
    small = [
        pltpu.make_async_copy(src, dst, sems.at[CHUNKS + c])
        for c, (src, dst) in enumerate(
            [
                (vol_hbm, vol_ref),
                (start_hbm, start_ref),
                (times_hbm, times_ref),
                (vol_hbm, vol_s),
                (outer_hbm, outer_ref),
            ]
        )
    ]
    for c in small + copies:
        c.start()
    for c in small[:4]:
        c.wait()
    vol_row = vol_ref[...]
    base = as_columns(jnp.log(start_ref[...]) + (drift - 0.5 * vol_row * vol_row), rows)
    vol = as_columns(vol_row, rows)
    times = times_ref[...]
    root_tau = jnp.sqrt(1.0 - times)
    inverse = 1.0 / root_tau
    ratio = jnp.sqrt(times) * inverse
    small[4].wait()
    for r, n in row_tiles(rows):
        drifted = base[r : r + n] * inverse
        level_v[r : r + n, :] = drifted + (vol[r : r + n] * ratio) * outer_ref[r : r + n, :].astype(F32)

    def level(d):
        return level_v[pl.ds(d, 1), :] + vol_s[0, d] * noise_v[d].astype(F32)

    low = jnp.full((paths, points), jnp.inf, F32)
    for (lo, hi), c in zip(spans, copies):
        c.wait()
        size = hi - lo
        whole = size // STEP

        def body(t, low, lo=lo):
            for j in range(STEP):
                low = jnp.minimum(low, level(lo + t * STEP + j))
            return low

        low = lax.fori_loop(0, whole, body, low)
        for d in range(lo + whole * STEP, hi):
            low = jnp.minimum(low, level(d))
    out_ref[...] = low * root_tau


def split(value):
    parts = []
    for _ in range(3):
        part = value.astype(jnp.bfloat16)
        value = value - part.astype(F32)
        parts.append(part)
    return parts


def owner(z, step, zs):
    half = zs // 2
    if step < half:
        return z ^ step
    turn = step - half
    up, down = half + (z + turn) % half, (z - half + turn + 1) % half
    if isinstance(z, int):
        return up if z < half else down
    return jnp.where(z < half, up, down)


def parts_kernel(zs, noise_ref, out_ref):
    paths, rows, points = noise_ref.shape
    me = lax.axis_index("path")
    z, y = me // 2, me % 2
    for s in range(zs):
        columns = pl.ds(pl.multiple_of(owner(z, s, zs) * LANES, LANES), LANES)

        def tile(k, r):
            n = min(16, rows - r)
            if n <= 0:
                return jnp.zeros((16, LANES), F32)
            part = noise_ref[k, r : r + n, columns].astype(F32)
            if n < 16:
                part = jnp.concatenate([part, jnp.zeros((16 - n, LANES), F32)], axis=0)
            return part

        for k in range(paths):
            for r in range(0, LANES, 16):
                top, bottom = tile(k, r), tile(k, LANES + r)
                out_ref[k, 2 * s + y, r : r + 16, :] = pack_low(top, bottom)
                out_ref[k, 2 * s + 1 - y, r : r + 16, :] = pack_high(top, bottom)


def moments_kernel(zs, lows_ref, last_ref, parts_ref, times_ref, *rest):
    half = zs // 2
    send_far, keep_far, keep_near = rest[:3]
    send_near = rest[3 : 2 + half]
    pay, term = rest[2 + half :]
    paths, points = lows_ref.shape
    me = lax.axis_index("path")
    z = me // 2
    first = me % 2 == 0
    payoff = jnp.exp(jnp.minimum(lows_ref[...], last_ref[...]))
    pay[...] = payoff
    totals = jnp.sum(payoff, axis=0, keepdims=True)
    for s in range(zs):
        columns = pl.ds(pl.multiple_of(owner(z, s, zs) * LANES, LANES), LANES)
        both = jnp.concatenate([pay[:, columns], jnp.sqrt(1.0 - times_ref[0:1, columns])], axis=0)
        low, high = pack_low(both, both), pack_high(both, both)
        if s >= half:
            at = past = (s - half) * LANES
            same, other = keep_far, send_far
        else:
            at, past = 0, LANES
            same = other = keep_near if s == 0 else send_near[s - 1]
        for side, (ref, place) in enumerate(((same, at), (other, past))):
            rows = jnp.where(first, low, high) if side == 0 else jnp.where(first, high, low)
            weights = [jnp.broadcast_to(rows[k : k + 1], (8, LANES)) for k in range(paths + 1)]
            for r in range(0, LANES, 8):
                total = weights[0] * parts_ref[0, 2 * s + side, r : r + 8, :]
                for k in range(1, paths):
                    total = total + weights[k] * parts_ref[k, 2 * s + side, r : r + 8, :]
                ref[place + r : place + r + 8, :] = total
                if s == 0 and side == 0:
                    term[r : r + 8, :] = weights[paths] * total
                else:
                    term[r : r + 8, :] += weights[paths] * total
    extras = [totals[:, c : c + LANES] for c in range(0, points, LANES)]
    lanes_of = lax.broadcasted_iota(jnp.int32, (16, LANES), 1) // HALF
    picks = (lax.broadcasted_iota(jnp.int32, (16, LANES), 0) == lanes_of).astype(F32).astype(jnp.bfloat16)
    sums = sum(
        lax.dot_general(picks, part, (((1,), (1,)), ((), ())), preferred_element_type=F32)
        for part in split(term[...])
    )
    extras.append(sums[0 : EXTRA - len(extras), :])
    extras = jnp.concatenate(extras, axis=0)
    for ref in (send_far, keep_far, *send_near):
        ref[ref.shape[0] - EXTRA :, :] = extras
    keep_near[2 * LANES :, :] = jnp.zeros((EXTRA, LANES), F32)


def scale_kernel(inner_total, outer_ref, start_ref, vol_ref, times_ref, out_ref):
    rows = outer_ref.shape[0]
    me = lax.axis_index("path")
    z = me // 2
    first = me % 2 == 0
    columns = pl.ds(pl.multiple_of(z * LANES, LANES), LANES)

    def pack(top, bottom):
        return jnp.where(first, pack_low(top, bottom), pack_high(top, bottom))

    vol = as_columns(vol_ref[...], rows)
    start = as_columns(start_ref[...], rows)
    spare = jnp.zeros((2 * LANES - rows, LANES), F32)
    outer = outer_ref[:, columns].astype(F32)
    outer = pack(outer[0:LANES], jnp.concatenate([outer[LANES:rows], spare], axis=0))
    times = times_ref[0:1, columns]
    times = pack(times, times)
    side = low_lanes((LANES, LANES))
    vol = jnp.where(side, vol[0:LANES], vol[LANES:])
    start = jnp.where(side, start[0:LANES], start[LANES:])
    state = start * jnp.exp((drift - 0.5 * vol * vol) * times + vol * jnp.sqrt(times) * outer)
    out_ref[...] = 1.0 / (inner_total * vol * state * jnp.sqrt(1.0 - times))


def final_kernel(
    inner_total, n_parts, near_ref, far_extra_ref, scale_ref, outer_ref, start_ref, vol_ref, times_ref, *rest
):
    parts, (value_ref, grad_ref, point_ref, point_grad_ref) = rest[:n_parts], rest[n_parts:]
    rows, points = outer_ref.shape
    me = lax.axis_index("path")
    first = me % 2 == 0
    moments = near_ref[0:LANES, :]
    extra = far_extra_ref[...] + near_ref[2 * LANES : 2 * LANES + EXTRA, :]
    for part in parts:
        moments = moments + part[0:LANES, :]
        extra = extra + part[LANES : LANES + EXTRA, :]
    grad = moments * scale_ref[...]
    turned = jnp.transpose(grad)
    point_grad_ref[:, 0:LANES] = turned[0:HALF]
    point_grad_ref[:, LANES:rows] = turned[HALF:, 0 : rows - LANES]
    blocks = points // LANES
    totals = jnp.concatenate([extra[c : c + 1, :] for c in range(blocks)], axis=1)
    inner_term = jnp.concatenate([extra[blocks : blocks + 1, :], extra[blocks + 1 : blocks + 2, :]], axis=1)
    values = totals / inner_total
    driver = driver_of(values)
    value_ref[...] = jnp.sum(totals, axis=1, keepdims=True) / (points * inner_total) + (
        jnp.sum(driver, axis=1, keepdims=True) / points
    )
    own = extra[0:1, :]
    for c in range(1, blocks):
        own = jnp.where(me // 2 == c, extra[c : c + 1, :], own)
    own = jnp.where(first, own, swap_halves(own)) / inner_total
    point_ref[...] = own[:, 0:HALF]
    root_times = jnp.sqrt(times_ref[...])
    weight = totals * root_times / inner_total + driver / root_times
    parts_of = [part.astype(F32) for part in split(weight)]
    weights = jnp.concatenate(parts_of + [jnp.zeros((13, points), F32)], axis=0).astype(jnp.bfloat16)
    outer_term = jnp.sum(
        lax.dot_general(
            weights, outer_ref[...], (((1,), (1,)), ((), ())), preferred_element_type=F32
        ),
        axis=0,
        keepdims=True,
    )
    grad_ref[...] = (inner_term[:, 0:rows] / inner_total + outer_term) / (
        points * vol_ref[...] * start_ref[...]
    )


def paired(inner_noise, outer_noise, start, vol, times):
    paths, rows, points = inner_noise.shape
    groups, dims = lax.axis_size("path"), lax.axis_size("dim")
    inner_total = paths * groups
    zs = groups // 2
    half = zs // 2
    start_row, vol_row, times_row = start[None, :], vol[None, :], times[None, :]
    limit = pltpu.CompilerParams(vmem_limit_bytes=16 * 1024 * 1024)

    lows, held_noise = pl.pallas_call(
        minima_kernel,
        out_shape=(
            pltpu.VMEM((paths, points), F32),
            pltpu.VMEM((rows, paths, points), inner_noise.dtype),
        ),
        in_specs=[pl.BlockSpec(memory_space=pltpu.HBM)] * 5,
        scratch_shapes=[
            pltpu.VMEM((rows, points), outer_noise.dtype),
            pltpu.VMEM((1, rows), F32),
            pltpu.VMEM((1, rows), F32),
            pltpu.VMEM((1, points), F32),
            pltpu.SMEM((1, rows), F32),
            pltpu.VMEM((rows, points), F32),
            pltpu.SemaphoreType.DMA((CHUNKS + 5,)),
        ],
        compiler_params=limit,
        name="minima",
    )(*[
        pltpu.with_memory_space_constraint(x, pltpu.HBM)
        for x in (jnp.transpose(inner_noise, (1, 0, 2)), outer_noise, start_row, vol_row, times_row)
    ])
    held_noise = jnp.transpose(held_noise, (1, 0, 2))

    last = None
    for bit in [1 << n for n in range(dims.bit_length() - 1)]:
        if last is not None:
            lows = jnp.minimum(lows, last)
        last = lax.ppermute(lows, "dim", [(i, i ^ bit) for i in range(dims)])

    parts = pl.pallas_call(
        functools.partial(parts_kernel, zs),
        out_shape=pltpu.VMEM((paths, 2 * zs, LANES, LANES), F32),
        compiler_params=limit,
        cost_estimate=pl.CostEstimate(
            flops=paths * rows * points, bytes_accessed=6 * paths * rows * points, transcendentals=0
        ),
        name="parts",
    )(held_noise)

    send_far, keep_far, keep_near, *send_near = pl.pallas_call(
        functools.partial(moments_kernel, zs),
        out_shape=[pltpu.VMEM((half * LANES + EXTRA, LANES), F32)] * 2
        + [pltpu.VMEM((2 * LANES + EXTRA, LANES), F32)] * half,
        scratch_shapes=[pltpu.VMEM((paths, points), F32), pltpu.VMEM((LANES, LANES), F32)],
        compiler_params=limit,
        name="moments",
    )(lows, last, parts, times_row)

    def along_z(message, step):
        route = [(i, 2 * owner(i // 2, step, zs) + i % 2) for i in range(groups)]
        return lax.ppermute(message, "path", route)

    def along_y(message):
        return lax.ppermute(message, "path", [(i, i ^ 1) for i in range(groups)])

    far_sum = keep_far + along_y(send_far)
    near_sum = keep_near
    for step in range(1, half):
        near_sum = near_sum + along_z(send_near[step - 1], step)
    scale = pl.pallas_call(
        functools.partial(scale_kernel, inner_total),
        out_shape=pltpu.VMEM((LANES, LANES), F32),
        compiler_params=limit,
        name="scale",
    )(outer_noise, start_row, vol_row, times_row)
    far_extra = far_sum[half * LANES :]
    arrived = []
    for n in range(half):
        message = jnp.concatenate([far_sum[n * LANES : (n + 1) * LANES], far_extra], axis=0)
        arrived.append(along_z(message, half + n))
    arrived.append(along_y(near_sum[LANES:]))

    value, grad, point, point_grad = pl.pallas_call(
        functools.partial(final_kernel, inner_total, len(arrived)),
        out_shape=[
            jax.ShapeDtypeStruct((1, 1), F32),
            jax.ShapeDtypeStruct((1, rows), F32),
            jax.ShapeDtypeStruct((1, points // groups), F32),
            jax.ShapeDtypeStruct((points // groups, rows), F32),
        ],
        compiler_params=limit,
        name="final",
    )(near_sum, far_extra, scale, outer_noise, start_row, vol_row, times_row, *arrived)
    return value.reshape(1), grad.reshape(rows), point.reshape(points // groups), jnp.transpose(point_grad)


def per_device(inner_noise, outer_noise, start, vol, times):
    rows, points = outer_noise.shape
    groups, dims = lax.axis_size("path"), lax.axis_size("dim")
    fits = (
        2 * points == LANES * groups
        and LANES < rows <= 2 * LANES
        and is_power(groups)
        and groups >= 4
        and is_power(dims)
        and dims > 1
        and points // LANES + 2 <= EXTRA
    )
    return (paired if fits else general)(inner_noise, outer_noise, start, vol, times)


def solution(mesh):
    in_specs = (P("path", "dim", None), P("dim", None), P("dim"), P("dim"), P())
    out_specs = (P(), P("dim"), P("path"), P("dim", "path"))
    return jax.shard_map(
        per_device, mesh=mesh, in_specs=in_specs, out_specs=out_specs, check_vma=False
    )
```

```python
import functools

import jax
import jax.numpy as jnp
from jax import lax
from jax.experimental import pallas as pl
from jax.experimental.pallas import tpu as pltpu
from jax.sharding import PartitionSpec as P

drift = 0.02
delta = 2.0 / 3.0
rate_free = 0.02
gamma_high = 0.2
gamma_low = 0.02
value_high = 0.4
value_low = 0.7

LANES = 128
HALF = LANES // 2
EXTRA = 8
CHUNKS = 8
STEP = 16
F32 = jnp.float32


def driver_of(value):
    slope = jnp.clip((value - value_high) / (value_low - value_high), 0.0, 1.0)
    quota = gamma_high + (gamma_low - gamma_high) * slope
    return -(1.0 - delta) * quota * value - rate_free * value


def is_power(n):
    return n > 0 and n & (n - 1) == 0


def general(inner_noise, outer_noise, start, vol, times):
    paths_here = inner_noise.shape[0]
    points = times.shape[0]
    groups = lax.axis_size("path")
    inner_total = paths_here * groups
    owned = points // groups
    tau = 1.0 - times
    outer = outer_noise.astype(F32)
    mean_rate = (drift - 0.5 * vol * vol)[:, None]
    outer_state = start[:, None] * jnp.exp(
        mean_rate * times[None, :] + vol[:, None] * jnp.sqrt(times)[None, :] * outer
    )
    shock = inner_noise.astype(F32)
    level = outer_state[None] * jnp.exp(
        (mean_rate * tau[None, :])[None] + (vol[:, None] * jnp.sqrt(tau)[None, :])[None] * shock
    )
    payoff = lax.pmin(jnp.min(level, axis=1), "dim")
    totals = jnp.sum(payoff, axis=0)
    moments = jnp.sum(payoff[:, None, :] * shock, axis=0)
    start_index = lax.axis_index("path") * owned
    totals, moments = lax.psum((totals, moments), "path")
    point_value = totals / inner_total
    point_grad_all = moments / (inner_total * vol[:, None] * outer_state * jnp.sqrt(tau)[None, :])
    driver = driver_of(point_value)
    root_value = jnp.sum(totals) / (points * inner_total) + jnp.sum(driver) / points
    terminal = jnp.sum(
        jnp.sqrt(times)[None, :] * outer * totals[None, :] + jnp.sqrt(tau)[None, :] * moments,
        axis=1,
    )
    integral = jnp.sum(driver[None, :] * outer / jnp.sqrt(times)[None, :], axis=1)
    root_grad = terminal / (points * inner_total * vol * start) + integral / (points * vol * start)
    own_value = lax.dynamic_slice_in_dim(point_value, start_index, owned, 0)
    own_grad = lax.dynamic_slice_in_dim(point_grad_all, start_index, owned, 1)
    return (jnp.reshape(root_value, (1,)), root_grad, own_value, own_grad)


def row_tiles(rows):
    return [(r, min(16, rows - r)) for r in range(0, rows, 16)]


def as_columns(row, rows):
    full = -(-rows // LANES) * LANES
    row = jnp.concatenate([row, jnp.ones((1, full - rows), F32)], axis=1)
    return jnp.transpose(jnp.broadcast_to(row, (8, full)))[:, 0:1]


def swap_halves(block):
    return pltpu.roll(block, HALF, 1)


def low_lanes(shape):
    return lax.broadcasted_iota(jnp.int32, shape, 1) < HALF


def pack_low(top, bottom):
    return jnp.where(low_lanes(top.shape), top, swap_halves(bottom))


def pack_high(top, bottom):
    return jnp.where(low_lanes(top.shape), swap_halves(top), bottom)


def minima_kernel(
    noise_hbm, outer_hbm, start_hbm, vol_hbm, times_hbm, out_ref, noise_v,
    outer_ref, start_ref, vol_ref, times_ref, vol_s, level_v, sems,
):
    rows, paths, points = noise_hbm.shape
    cuts = [rows * c // CHUNKS // 16 * 16 for c in range(CHUNKS)] + [rows]
    spans = list(zip(cuts[:-1], cuts[1:]))
    copies = [
        pltpu.make_async_copy(noise_hbm.at[lo:hi], noise_v.at[lo:hi], sems.at[c])
        for c, (lo, hi) in enumerate(spans)
    ]
    small = [
        pltpu.make_async_copy(src, dst, sems.at[CHUNKS + c])
        for c, (src, dst) in enumerate(
            [
                (vol_hbm, vol_ref),
                (start_hbm, start_ref),
                (times_hbm, times_ref),
                (vol_hbm, vol_s),
                (outer_hbm, outer_ref),
            ]
        )
    ]
    for c in small + copies:
        c.start()
    for c in small[:4]:
        c.wait()
    vol_row = vol_ref[...]
    base = as_columns(jnp.log(start_ref[...]) + (drift - 0.5 * vol_row * vol_row), rows)
    vol = as_columns(vol_row, rows)
    times = times_ref[...]
    root_tau = jnp.sqrt(1.0 - times)
    inverse = 1.0 / root_tau
    ratio = jnp.sqrt(times) * inverse
    small[4].wait()
    for r, n in row_tiles(rows):
        drifted = base[r : r + n] * inverse
        level_v[r : r + n, :] = drifted + (vol[r : r + n] * ratio) * outer_ref[r : r + n, :].astype(F32)

    def level(d):
        return level_v[pl.ds(d, 1), :] + vol_s[0, d] * noise_v[d].astype(F32)

    low = jnp.full((paths, points), jnp.inf, F32)
    for (lo, hi), c in zip(spans, copies):
        c.wait()
        size = hi - lo
        whole = size // STEP

        def body(t, low, lo=lo):
            for j in range(STEP):
                low = jnp.minimum(low, level(lo + t * STEP + j))
            return low

        low = lax.fori_loop(0, whole, body, low)
        for d in range(lo + whole * STEP, hi):
            low = jnp.minimum(low, level(d))
    out_ref[...] = low * root_tau


def split(value):
    parts = []
    for _ in range(3):
        part = value.astype(jnp.bfloat16)
        value = value - part.astype(F32)
        parts.append(part)
    return parts


def owner(z, step, zs):
    half = zs // 2
    if step < half:
        return z ^ step
    turn = step - half
    up, down = half + (z + turn) % half, (z - half + turn + 1) % half
    if isinstance(z, int):
        return up if z < half else down
    return jnp.where(z < half, up, down)


def parts_kernel(zs, noise_ref, out_ref):
    paths, rows, points = noise_ref.shape
    me = lax.axis_index("path")
    z, y = me // 2, me % 2
    for s in range(zs):
        columns = pl.ds(pl.multiple_of(owner(z, s, zs) * LANES, LANES), LANES)

        def tile(k, r):
            n = min(16, rows - r)
            if n <= 0:
                return jnp.zeros((16, LANES), F32)
            part = noise_ref[k, r : r + n, columns].astype(F32)
            if n < 16:
                part = jnp.concatenate([part, jnp.zeros((16 - n, LANES), F32)], axis=0)
            return part

        for k in range(paths):
            for r in range(0, LANES, 16):
                top, bottom = tile(k, r), tile(k, LANES + r)
                out_ref[k, 2 * s + y, r : r + 16, :] = pack_low(top, bottom)
                out_ref[k, 2 * s + 1 - y, r : r + 16, :] = pack_high(top, bottom)


def moments_kernel(zs, n_lows, *refs):
    half = zs // 2
    lows, (parts_ref, times_ref, *rest) = refs[:n_lows], refs[n_lows:]
    send_far, keep_far, keep_near = rest[:3]
    send_near = rest[3 : 2 + half]
    pay, term = rest[2 + half :]
    paths, points = lows[0].shape
    me = lax.axis_index("path")
    z = me // 2
    first = me % 2 == 0
    payoff = jnp.exp(functools.reduce(jnp.minimum, [low[...] for low in lows]))
    pay[...] = payoff
    totals = jnp.sum(payoff, axis=0, keepdims=True)
    for s in range(zs):
        columns = pl.ds(pl.multiple_of(owner(z, s, zs) * LANES, LANES), LANES)
        both = jnp.concatenate([pay[:, columns], jnp.sqrt(1.0 - times_ref[0:1, columns])], axis=0)
        low, high = pack_low(both, both), pack_high(both, both)
        if s >= half:
            at = past = (s - half) * LANES
            same, other = keep_far, send_far
        else:
            at, past = 0, LANES
            same = other = keep_near if s == 0 else send_near[s - 1]
        for side, (ref, place) in enumerate(((same, at), (other, past))):
            rows = jnp.where(first, low, high) if side == 0 else jnp.where(first, high, low)
            weights = [jnp.broadcast_to(rows[k : k + 1], (8, LANES)) for k in range(paths + 1)]
            for r in range(0, LANES, 8):
                total = weights[0] * parts_ref[0, 2 * s + side, r : r + 8, :]
                for k in range(1, paths):
                    total = total + weights[k] * parts_ref[k, 2 * s + side, r : r + 8, :]
                ref[place + r : place + r + 8, :] = total
                if s == 0 and side == 0:
                    term[r : r + 8, :] = weights[paths] * total
                else:
                    term[r : r + 8, :] += weights[paths] * total
    extras = [totals[:, c : c + LANES] for c in range(0, points, LANES)]
    lanes_of = lax.broadcasted_iota(jnp.int32, (16, LANES), 1) // HALF
    picks = (lax.broadcasted_iota(jnp.int32, (16, LANES), 0) == lanes_of).astype(F32).astype(jnp.bfloat16)
    sums = sum(
        lax.dot_general(picks, part, (((1,), (1,)), ((), ())), preferred_element_type=F32)
        for part in split(term[...])
    )
    extras.append(sums[0 : EXTRA - len(extras), :])
    extras = jnp.concatenate(extras, axis=0)
    for ref in (send_far, keep_far, *send_near):
        ref[ref.shape[0] - EXTRA :, :] = extras
    keep_near[2 * LANES :, :] = jnp.zeros((EXTRA, LANES), F32)


def scale_kernel(inner_total, outer_ref, start_ref, vol_ref, times_ref, out_ref):
    rows = outer_ref.shape[0]
    me = lax.axis_index("path")
    z = me // 2
    first = me % 2 == 0
    columns = pl.ds(pl.multiple_of(z * LANES, LANES), LANES)

    def pack(top, bottom):
        return jnp.where(first, pack_low(top, bottom), pack_high(top, bottom))

    vol = as_columns(vol_ref[...], rows)
    start = as_columns(start_ref[...], rows)
    spare = jnp.zeros((2 * LANES - rows, LANES), F32)
    outer = outer_ref[:, columns].astype(F32)
    outer = pack(outer[0:LANES], jnp.concatenate([outer[LANES:rows], spare], axis=0))
    times = times_ref[0:1, columns]
    times = pack(times, times)
    side = low_lanes((LANES, LANES))
    vol = jnp.where(side, vol[0:LANES], vol[LANES:])
    start = jnp.where(side, start[0:LANES], start[LANES:])
    state = start * jnp.exp((drift - 0.5 * vol * vol) * times + vol * jnp.sqrt(times) * outer)
    out_ref[...] = 1.0 / (inner_total * vol * state * jnp.sqrt(1.0 - times))


def final_kernel(
    inner_total, n_parts, near_ref, far_extra_ref, scale_ref, outer_ref, start_ref, vol_ref, times_ref, *rest
):
    parts, (value_ref, grad_ref, point_ref, point_grad_ref) = rest[:n_parts], rest[n_parts:]
    rows, points = outer_ref.shape
    me = lax.axis_index("path")
    first = me % 2 == 0
    moments = near_ref[0:LANES, :]
    extra = far_extra_ref[...] + near_ref[2 * LANES : 2 * LANES + EXTRA, :]
    for part in parts:
        moments = moments + part[0:LANES, :]
        extra = extra + part[LANES : LANES + EXTRA, :]
    grad = moments * scale_ref[...]
    turned = jnp.transpose(grad)
    point_grad_ref[:, 0:LANES] = turned[0:HALF]
    point_grad_ref[:, LANES:rows] = turned[HALF:, 0 : rows - LANES]
    blocks = points // LANES
    totals = jnp.concatenate([extra[c : c + 1, :] for c in range(blocks)], axis=1)
    inner_term = jnp.concatenate([extra[blocks : blocks + 1, :], extra[blocks + 1 : blocks + 2, :]], axis=1)
    values = totals / inner_total
    driver = driver_of(values)
    value_ref[...] = jnp.sum(totals, axis=1, keepdims=True) / (points * inner_total) + (
        jnp.sum(driver, axis=1, keepdims=True) / points
    )
    own = extra[0:1, :]
    for c in range(1, blocks):
        own = jnp.where(me // 2 == c, extra[c : c + 1, :], own)
    own = jnp.where(first, own, swap_halves(own)) / inner_total
    point_ref[...] = own[:, 0:HALF]
    root_times = jnp.sqrt(times_ref[...])
    weight = totals * root_times / inner_total + driver / root_times
    parts_of = [part.astype(F32) for part in split(weight)]
    weights = jnp.concatenate(parts_of + [jnp.zeros((13, points), F32)], axis=0).astype(jnp.bfloat16)
    outer_term = jnp.sum(
        lax.dot_general(
            weights, outer_ref[...], (((1,), (1,)), ((), ())), preferred_element_type=F32
        ),
        axis=0,
        keepdims=True,
    )
    grad_ref[...] = (inner_term[:, 0:rows] / inner_total + outer_term) / (
        points * vol_ref[...] * start_ref[...]
    )


def paired(inner_noise, outer_noise, start, vol, times):
    paths, rows, points = inner_noise.shape
    groups, dims = lax.axis_size("path"), lax.axis_size("dim")
    inner_total = paths * groups
    zs = groups // 2
    half = zs // 2
    start_row, vol_row, times_row = start[None, :], vol[None, :], times[None, :]
    limit = pltpu.CompilerParams(vmem_limit_bytes=16 * 1024 * 1024)

    lows, held_noise = pl.pallas_call(
        minima_kernel,
        out_shape=(
            pltpu.VMEM((paths, points), F32),
            pltpu.VMEM((rows, paths, points), inner_noise.dtype),
        ),
        in_specs=[pl.BlockSpec(memory_space=pltpu.HBM)] * 5,
        scratch_shapes=[
            pltpu.VMEM((rows, points), outer_noise.dtype),
            pltpu.VMEM((1, rows), F32),
            pltpu.VMEM((1, rows), F32),
            pltpu.VMEM((1, points), F32),
            pltpu.SMEM((1, rows), F32),
            pltpu.VMEM((rows, points), F32),
            pltpu.SemaphoreType.DMA((CHUNKS + 5,)),
        ],
        compiler_params=limit,
        name="minima",
    )(*[
        pltpu.with_memory_space_constraint(x, pltpu.HBM)
        for x in (jnp.transpose(inner_noise, (1, 0, 2)), outer_noise, start_row, vol_row, times_row)
    ])
    held_noise = jnp.transpose(held_noise, (1, 0, 2))

    others = [
        lax.ppermute(lows, "dim", [(i, i ^ s) for i in range(dims)])
        for s in sorted(range(1, dims), key=lambda s: (s < 2, s))
    ]

    parts = pl.pallas_call(
        functools.partial(parts_kernel, zs),
        out_shape=pltpu.VMEM((paths, 2 * zs, LANES, LANES), F32),
        compiler_params=limit,
        cost_estimate=pl.CostEstimate(
            flops=paths * rows * points, bytes_accessed=6 * paths * rows * points, transcendentals=0
        ),
        name="parts",
    )(held_noise)

    send_far, keep_far, keep_near, *send_near = pl.pallas_call(
        functools.partial(moments_kernel, zs, dims),
        out_shape=[pltpu.VMEM((half * LANES + EXTRA, LANES), F32)] * 2
        + [pltpu.VMEM((2 * LANES + EXTRA, LANES), F32)] * half,
        scratch_shapes=[pltpu.VMEM((paths, points), F32), pltpu.VMEM((LANES, LANES), F32)],
        compiler_params=limit,
        name="moments",
    )(lows, *others, parts, times_row)

    def along_z(message, step):
        route = [(i, 2 * owner(i // 2, step, zs) + i % 2) for i in range(groups)]
        return lax.ppermute(message, "path", route)

    def along_y(message):
        return lax.ppermute(message, "path", [(i, i ^ 1) for i in range(groups)])

    far_sum = keep_far + along_y(send_far)
    near_sum = keep_near
    for step in range(1, half):
        near_sum = near_sum + along_z(send_near[step - 1], step)
    scale = pl.pallas_call(
        functools.partial(scale_kernel, inner_total),
        out_shape=pltpu.VMEM((LANES, LANES), F32),
        compiler_params=limit,
        name="scale",
    )(outer_noise, start_row, vol_row, times_row)
    far_extra = far_sum[half * LANES :]
    arrived = []
    for n in range(half):
        message = jnp.concatenate([far_sum[n * LANES : (n + 1) * LANES], far_extra], axis=0)
        arrived.append(along_z(message, half + n))
    arrived.append(along_y(near_sum[LANES:]))

    value, grad, point, point_grad = pl.pallas_call(
        functools.partial(final_kernel, inner_total, len(arrived)),
        out_shape=[
            jax.ShapeDtypeStruct((1, 1), F32),
            jax.ShapeDtypeStruct((1, rows), F32),
            jax.ShapeDtypeStruct((1, points // groups), F32),
            jax.ShapeDtypeStruct((points // groups, rows), F32),
        ],
        compiler_params=limit,
        name="final",
    )(near_sum, far_extra, scale, outer_noise, start_row, vol_row, times_row, *arrived)
    return value.reshape(1), grad.reshape(rows), point.reshape(points // groups), jnp.transpose(point_grad)


def per_device(inner_noise, outer_noise, start, vol, times):
    rows, points = outer_noise.shape
    groups, dims = lax.axis_size("path"), lax.axis_size("dim")
    fits = (
        2 * points == LANES * groups
        and LANES < rows <= 2 * LANES
        and is_power(groups)
        and groups >= 4
        and is_power(dims)
        and dims > 1
        and points // LANES + 2 <= EXTRA
    )
    return (paired if fits else general)(inner_noise, outer_noise, start, vol, times)


def solution(mesh):
    in_specs = (P("path", "dim", None), P("dim", None), P("dim"), P("dim"), P())
    out_specs = (P(), P("dim"), P("path"), P("dim", "path"))
    return jax.shard_map(
        per_device, mesh=mesh, in_specs=in_specs, out_specs=out_specs, check_vma=False
    )
```

```python
import functools

import jax
import jax.numpy as jnp
from jax import lax
from jax.experimental import pallas as pl
from jax.experimental.pallas import tpu as pltpu
from jax.sharding import PartitionSpec as P

drift = 0.02
delta = 2.0 / 3.0
rate_free = 0.02
gamma_high = 0.2
gamma_low = 0.02
value_high = 0.4
value_low = 0.7

LANES = 128
HALF = LANES // 2
EXTRA = 8
CHUNKS = 8
STEP = 16
F32 = jnp.float32


def driver_of(value):
    slope = jnp.clip((value - value_high) / (value_low - value_high), 0.0, 1.0)
    quota = gamma_high + (gamma_low - gamma_high) * slope
    return -(1.0 - delta) * quota * value - rate_free * value


def is_power(n):
    return n > 0 and n & (n - 1) == 0


def general(inner_noise, outer_noise, start, vol, times):
    paths_here = inner_noise.shape[0]
    points = times.shape[0]
    groups = lax.axis_size("path")
    inner_total = paths_here * groups
    owned = points // groups
    tau = 1.0 - times
    outer = outer_noise.astype(F32)
    mean_rate = (drift - 0.5 * vol * vol)[:, None]
    outer_state = start[:, None] * jnp.exp(
        mean_rate * times[None, :] + vol[:, None] * jnp.sqrt(times)[None, :] * outer
    )
    shock = inner_noise.astype(F32)
    level = outer_state[None] * jnp.exp(
        (mean_rate * tau[None, :])[None] + (vol[:, None] * jnp.sqrt(tau)[None, :])[None] * shock
    )
    payoff = lax.pmin(jnp.min(level, axis=1), "dim")
    totals = jnp.sum(payoff, axis=0)
    moments = jnp.sum(payoff[:, None, :] * shock, axis=0)
    start_index = lax.axis_index("path") * owned
    totals, moments = lax.psum((totals, moments), "path")
    point_value = totals / inner_total
    point_grad_all = moments / (inner_total * vol[:, None] * outer_state * jnp.sqrt(tau)[None, :])
    driver = driver_of(point_value)
    root_value = jnp.sum(totals) / (points * inner_total) + jnp.sum(driver) / points
    terminal = jnp.sum(
        jnp.sqrt(times)[None, :] * outer * totals[None, :] + jnp.sqrt(tau)[None, :] * moments,
        axis=1,
    )
    integral = jnp.sum(driver[None, :] * outer / jnp.sqrt(times)[None, :], axis=1)
    root_grad = terminal / (points * inner_total * vol * start) + integral / (points * vol * start)
    own_value = lax.dynamic_slice_in_dim(point_value, start_index, owned, 0)
    own_grad = lax.dynamic_slice_in_dim(point_grad_all, start_index, owned, 1)
    return (jnp.reshape(root_value, (1,)), root_grad, own_value, own_grad)


def row_tiles(rows):
    return [(r, min(16, rows - r)) for r in range(0, rows, 16)]


def as_columns(row, rows):
    full = -(-rows // LANES) * LANES
    row = jnp.concatenate([row, jnp.ones((1, full - rows), F32)], axis=1)
    return jnp.transpose(jnp.broadcast_to(row, (8, full)))[:, 0:1]


def swap_halves(block):
    return pltpu.roll(block, HALF, 1)


def low_lanes(shape):
    return lax.broadcasted_iota(jnp.int32, shape, 1) < HALF


def pack_low(top, bottom):
    return jnp.where(low_lanes(top.shape), top, swap_halves(bottom))


def pack_high(top, bottom):
    return jnp.where(low_lanes(top.shape), swap_halves(top), bottom)


def minima_kernel(
    noise_hbm, outer_hbm, start_hbm, vol_hbm, times_hbm, out_ref, noise_v,
    outer_ref, start_ref, vol_ref, times_ref, vol_s, level_v, sems,
):
    rows, paths, points = noise_hbm.shape
    cuts = [rows * c // CHUNKS // 16 * 16 for c in range(CHUNKS)] + [rows]
    spans = list(zip(cuts[:-1], cuts[1:]))
    copies = [
        pltpu.make_async_copy(noise_hbm.at[lo:hi], noise_v.at[lo:hi], sems.at[c])
        for c, (lo, hi) in enumerate(spans)
    ]
    small = [
        pltpu.make_async_copy(src, dst, sems.at[CHUNKS + c])
        for c, (src, dst) in enumerate(
            [
                (vol_hbm, vol_ref),
                (start_hbm, start_ref),
                (times_hbm, times_ref),
                (vol_hbm, vol_s),
                (outer_hbm, outer_ref),
            ]
        )
    ]
    for c in small + copies:
        c.start()
    for c in small[:4]:
        c.wait()
    vol_row = vol_ref[...]
    base = as_columns(jnp.log(start_ref[...]) + (drift - 0.5 * vol_row * vol_row), rows)
    vol = as_columns(vol_row, rows)
    times = times_ref[...]
    root_tau = jnp.sqrt(1.0 - times)
    inverse = 1.0 / root_tau
    ratio = jnp.sqrt(times) * inverse
    small[4].wait()
    for r, n in row_tiles(rows):
        drifted = base[r : r + n] * inverse
        level_v[r : r + n, :] = drifted + (vol[r : r + n] * ratio) * outer_ref[r : r + n, :].astype(F32)

    def level(d):
        return level_v[pl.ds(d, 1), :] + vol_s[0, d] * noise_v[d].astype(F32)

    low = jnp.full((paths, points), jnp.inf, F32)
    for (lo, hi), c in zip(spans, copies):
        c.wait()
        size = hi - lo
        whole = size // STEP

        def body(t, low, lo=lo):
            for j in range(STEP):
                low = jnp.minimum(low, level(lo + t * STEP + j))
            return low

        low = lax.fori_loop(0, whole, body, low)
        for d in range(lo + whole * STEP, hi):
            low = jnp.minimum(low, level(d))
    out_ref[...] = low * root_tau


def split(value):
    parts = []
    for _ in range(3):
        part = value.astype(jnp.bfloat16)
        value = value - part.astype(F32)
        parts.append(part)
    return parts


def owner(z, step, zs):
    half = zs // 2
    if step < half:
        return z ^ step
    turn = step - half
    up, down = half + (z + turn) % half, (z - half + turn + 1) % half
    if isinstance(z, int):
        return up if z < half else down
    return jnp.where(z < half, up, down)


def parts_kernel(zs, noise_ref, out_ref):
    paths, rows, points = noise_ref.shape
    me = lax.axis_index("path")
    z, y = me // 2, me % 2
    for s in range(zs):
        columns = pl.ds(pl.multiple_of(owner(z, s, zs) * LANES, LANES), LANES)

        def tile(k, r):
            n = min(16, rows - r)
            if n <= 0:
                return jnp.zeros((16, LANES), F32)
            part = noise_ref[k, r : r + n, columns].astype(F32)
            if n < 16:
                part = jnp.concatenate([part, jnp.zeros((16 - n, LANES), F32)], axis=0)
            return part

        for k in range(paths):
            for r in range(0, LANES, 16):
                top, bottom = tile(k, r), tile(k, LANES + r)
                out_ref[k, 2 * s + y, r : r + 16, :] = pack_low(top, bottom)
                out_ref[k, 2 * s + 1 - y, r : r + 16, :] = pack_high(top, bottom)


def moments_kernel(zs, n_lows, *refs):
    half = zs // 2
    lows, (parts_ref, times_ref, *rest) = refs[:n_lows], refs[n_lows:]
    send_far, keep_far, keep_near = rest[:3]
    send_near = rest[3 : 2 + half]
    pay, term = rest[2 + half :]
    paths, points = lows[0].shape
    me = lax.axis_index("path")
    z = me // 2
    first = me % 2 == 0
    payoff = jnp.exp(functools.reduce(jnp.minimum, [low[...] for low in lows]))
    pay[...] = payoff
    totals = jnp.sum(payoff, axis=0, keepdims=True)
    for s in range(zs):
        columns = pl.ds(pl.multiple_of(owner(z, s, zs) * LANES, LANES), LANES)
        both = jnp.concatenate([pay[:, columns], jnp.sqrt(1.0 - times_ref[0:1, columns])], axis=0)
        low, high = pack_low(both, both), pack_high(both, both)
        if s >= half:
            at = past = (s - half) * LANES
            same, other = keep_far, send_far
        else:
            at, past = 0, LANES
            same = other = keep_near if s == 0 else send_near[s - 1]
        for side, (ref, place) in enumerate(((same, at), (other, past))):
            rows = jnp.where(first, low, high) if side == 0 else jnp.where(first, high, low)
            weights = [jnp.broadcast_to(rows[k : k + 1], (8, LANES)) for k in range(paths + 1)]
            for r in range(0, LANES, 8):
                total = weights[0] * parts_ref[0, 2 * s + side, r : r + 8, :]
                for k in range(1, paths):
                    total = total + weights[k] * parts_ref[k, 2 * s + side, r : r + 8, :]
                ref[place + r : place + r + 8, :] = total
                if s == 0 and side == 0:
                    term[r : r + 8, :] = weights[paths] * total
                else:
                    term[r : r + 8, :] += weights[paths] * total
    extras = [totals[:, c : c + LANES] for c in range(0, points, LANES)]
    lanes_of = lax.broadcasted_iota(jnp.int32, (16, LANES), 1) // HALF
    picks = (lax.broadcasted_iota(jnp.int32, (16, LANES), 0) == lanes_of).astype(F32).astype(jnp.bfloat16)
    sums = sum(
        lax.dot_general(picks, part, (((1,), (1,)), ((), ())), preferred_element_type=F32)
        for part in split(term[...])
    )
    extras.append(sums[0 : EXTRA - len(extras), :])
    extras = jnp.concatenate(extras, axis=0)
    for ref in (send_far, keep_far, *send_near):
        ref[ref.shape[0] - EXTRA :, :] = extras
    keep_near[2 * LANES :, :] = jnp.zeros((EXTRA, LANES), F32)


def join_kernel(keep_ref, got_ref, *messages):
    tail = keep_ref.shape[0] - EXTRA
    extras = keep_ref[tail:, :] + got_ref[tail:, :]
    for n, ref in enumerate(messages):
        block = slice(n * LANES, (n + 1) * LANES)
        ref[0:LANES, :] = keep_ref[block, :] + got_ref[block, :]
        ref[LANES:, :] = extras


def scale_kernel(inner_total, outer_ref, start_ref, vol_ref, times_ref, out_ref):
    rows = outer_ref.shape[0]
    me = lax.axis_index("path")
    z = me // 2
    first = me % 2 == 0
    columns = pl.ds(pl.multiple_of(z * LANES, LANES), LANES)

    def pack(top, bottom):
        return jnp.where(first, pack_low(top, bottom), pack_high(top, bottom))

    vol = as_columns(vol_ref[...], rows)
    start = as_columns(start_ref[...], rows)
    spare = jnp.zeros((2 * LANES - rows, LANES), F32)
    outer = outer_ref[:, columns].astype(F32)
    outer = pack(outer[0:LANES], jnp.concatenate([outer[LANES:rows], spare], axis=0))
    times = times_ref[0:1, columns]
    times = pack(times, times)
    side = low_lanes((LANES, LANES))
    vol = jnp.where(side, vol[0:LANES], vol[LANES:])
    start = jnp.where(side, start[0:LANES], start[LANES:])
    state = start * jnp.exp((drift - 0.5 * vol * vol) * times + vol * jnp.sqrt(times) * outer)
    out_ref[...] = 1.0 / (inner_total * vol * state * jnp.sqrt(1.0 - times))


def final_kernel(
    inner_total, n_parts, near_ref, far_extra_ref, scale_ref, outer_ref, start_ref, vol_ref, times_ref, *rest
):
    parts, (value_ref, grad_ref, point_ref, point_grad_ref) = rest[:n_parts], rest[n_parts:]
    rows, points = outer_ref.shape
    me = lax.axis_index("path")
    first = me % 2 == 0
    moments = near_ref[0:LANES, :]
    extra = far_extra_ref[...] + near_ref[2 * LANES : 2 * LANES + EXTRA, :]
    for part in parts:
        moments = moments + part[0:LANES, :]
        extra = extra + part[LANES : LANES + EXTRA, :]
    grad = moments * scale_ref[...]
    turned = jnp.transpose(grad)
    point_grad_ref[:, 0:LANES] = turned[0:HALF]
    point_grad_ref[:, LANES:rows] = turned[HALF:, 0 : rows - LANES]
    blocks = points // LANES
    totals = jnp.concatenate([extra[c : c + 1, :] for c in range(blocks)], axis=1)
    inner_term = jnp.concatenate([extra[blocks : blocks + 1, :], extra[blocks + 1 : blocks + 2, :]], axis=1)
    values = totals / inner_total
    driver = driver_of(values)
    value_ref[...] = jnp.sum(totals, axis=1, keepdims=True) / (points * inner_total) + (
        jnp.sum(driver, axis=1, keepdims=True) / points
    )
    own = extra[0:1, :]
    for c in range(1, blocks):
        own = jnp.where(me // 2 == c, extra[c : c + 1, :], own)
    own = jnp.where(first, own, swap_halves(own)) / inner_total
    point_ref[...] = own[:, 0:HALF]
    root_times = jnp.sqrt(times_ref[...])
    weight = totals * root_times / inner_total + driver / root_times
    parts_of = [part.astype(F32) for part in split(weight)]
    weights = jnp.concatenate(parts_of + [jnp.zeros((13, points), F32)], axis=0).astype(jnp.bfloat16)
    outer_term = jnp.sum(
        lax.dot_general(
            weights, outer_ref[...], (((1,), (1,)), ((), ())), preferred_element_type=F32
        ),
        axis=0,
        keepdims=True,
    )
    grad_ref[...] = (inner_term[:, 0:rows] / inner_total + outer_term) / (
        points * vol_ref[...] * start_ref[...]
    )


def paired(inner_noise, outer_noise, start, vol, times):
    paths, rows, points = inner_noise.shape
    groups, dims = lax.axis_size("path"), lax.axis_size("dim")
    inner_total = paths * groups
    zs = groups // 2
    half = zs // 2
    start_row, vol_row, times_row = start[None, :], vol[None, :], times[None, :]
    limit = pltpu.CompilerParams(vmem_limit_bytes=16 * 1024 * 1024)

    lows, held_noise = pl.pallas_call(
        minima_kernel,
        out_shape=(
            pltpu.VMEM((paths, points), F32),
            pltpu.VMEM((rows, paths, points), inner_noise.dtype),
        ),
        in_specs=[pl.BlockSpec(memory_space=pltpu.HBM)] * 5,
        scratch_shapes=[
            pltpu.VMEM((rows, points), outer_noise.dtype),
            pltpu.VMEM((1, rows), F32),
            pltpu.VMEM((1, rows), F32),
            pltpu.VMEM((1, points), F32),
            pltpu.SMEM((1, rows), F32),
            pltpu.VMEM((rows, points), F32),
            pltpu.SemaphoreType.DMA((CHUNKS + 5,)),
        ],
        compiler_params=limit,
        name="minima",
    )(*[
        pltpu.with_memory_space_constraint(x, pltpu.HBM)
        for x in (jnp.transpose(inner_noise, (1, 0, 2)), outer_noise, start_row, vol_row, times_row)
    ])
    held_noise = jnp.transpose(held_noise, (1, 0, 2))

    others = [
        lax.ppermute(lows, "dim", [(i, i ^ s) for i in range(dims)])
        for s in sorted(range(1, dims), key=lambda s: (s < 2, s))
    ]

    parts = pl.pallas_call(
        functools.partial(parts_kernel, zs),
        out_shape=pltpu.VMEM((paths, 2 * zs, LANES, LANES), F32),
        compiler_params=limit,
        cost_estimate=pl.CostEstimate(
            flops=paths * rows * points, bytes_accessed=6 * paths * rows * points, transcendentals=0
        ),
        name="parts",
    )(held_noise)

    send_far, keep_far, keep_near, *send_near = pl.pallas_call(
        functools.partial(moments_kernel, zs, dims),
        out_shape=[pltpu.VMEM((half * LANES + EXTRA, LANES), F32)] * 2
        + [pltpu.VMEM((2 * LANES + EXTRA, LANES), F32)] * half,
        scratch_shapes=[pltpu.VMEM((paths, points), F32), pltpu.VMEM((LANES, LANES), F32)],
        compiler_params=limit,
        name="moments",
    )(lows, *others, parts, times_row)

    def along_z(message, step):
        route = [(i, 2 * owner(i // 2, step, zs) + i % 2) for i in range(groups)]
        return lax.ppermute(message, "path", route)

    def along_y(message):
        return lax.ppermute(message, "path", [(i, i ^ 1) for i in range(groups)])

    messages = pl.pallas_call(
        join_kernel,
        out_shape=[pltpu.VMEM((LANES + EXTRA, LANES), F32)] * half,
        compiler_params=limit,
        name="join",
    )(keep_far, along_y(send_far))
    near_sum = keep_near
    for step in range(1, half):
        near_sum = near_sum + along_z(send_near[step - 1], step)
    scale = pl.pallas_call(
        functools.partial(scale_kernel, inner_total),
        out_shape=pltpu.VMEM((LANES, LANES), F32),
        compiler_params=limit,
        name="scale",
    )(outer_noise, start_row, vol_row, times_row)
    far_extra = messages[0][LANES:]
    arrived = [along_z(message, half + n) for n, message in enumerate(messages)]
    arrived.append(along_y(near_sum[LANES:]))

    value, grad, point, point_grad = pl.pallas_call(
        functools.partial(final_kernel, inner_total, len(arrived)),
        out_shape=[
            jax.ShapeDtypeStruct((1, 1), F32),
            jax.ShapeDtypeStruct((1, rows), F32),
            jax.ShapeDtypeStruct((1, points // groups), F32),
            jax.ShapeDtypeStruct((points // groups, rows), F32),
        ],
        compiler_params=limit,
        name="final",
    )(near_sum, far_extra, scale, outer_noise, start_row, vol_row, times_row, *arrived)
    return value.reshape(1), grad.reshape(rows), point.reshape(points // groups), jnp.transpose(point_grad)


def per_device(inner_noise, outer_noise, start, vol, times):
    rows, points = outer_noise.shape
    groups, dims = lax.axis_size("path"), lax.axis_size("dim")
    fits = (
        2 * points == LANES * groups
        and LANES < rows <= 2 * LANES
        and is_power(groups)
        and groups >= 4
        and is_power(dims)
        and dims > 1
        and points // LANES + 2 <= EXTRA
    )
    return (paired if fits else general)(inner_noise, outer_noise, start, vol, times)


def solution(mesh):
    in_specs = (P("path", "dim", None), P("dim", None), P("dim"), P("dim"), P())
    out_specs = (P(), P("dim"), P("path"), P("dim", "path"))
    return jax.shard_map(
        per_device, mesh=mesh, in_specs=in_specs, out_specs=out_specs, check_vma=False
    )
```

```python
import functools

import jax
import jax.numpy as jnp
from jax import lax
from jax.experimental import pallas as pl
from jax.experimental.pallas import tpu as pltpu
from jax.sharding import PartitionSpec as P

drift = 0.02
delta = 2.0 / 3.0
rate_free = 0.02
gamma_high = 0.2
gamma_low = 0.02
value_high = 0.4
value_low = 0.7

LANES = 128
HALF = LANES // 2
EXTRA = 8
CHUNKS = 8
STEP = 16
F32 = jnp.float32


def driver_of(value):
    slope = jnp.clip((value - value_high) * (1.0 / (value_low - value_high)), 0.0, 1.0)
    quota = gamma_high + (gamma_low - gamma_high) * slope
    return -(1.0 - delta) * quota * value - rate_free * value


def is_power(n):
    return n > 0 and n & (n - 1) == 0


def general(inner_noise, outer_noise, start, vol, times):
    paths_here = inner_noise.shape[0]
    points = times.shape[0]
    groups = lax.axis_size("path")
    inner_total = paths_here * groups
    owned = points // groups
    tau = 1.0 - times
    outer = outer_noise.astype(F32)
    mean_rate = (drift - 0.5 * vol * vol)[:, None]
    outer_state = start[:, None] * jnp.exp(
        mean_rate * times[None, :] + vol[:, None] * jnp.sqrt(times)[None, :] * outer
    )
    shock = inner_noise.astype(F32)
    level = outer_state[None] * jnp.exp(
        (mean_rate * tau[None, :])[None] + (vol[:, None] * jnp.sqrt(tau)[None, :])[None] * shock
    )
    payoff = lax.pmin(jnp.min(level, axis=1), "dim")
    totals = jnp.sum(payoff, axis=0)
    moments = jnp.sum(payoff[:, None, :] * shock, axis=0)
    start_index = lax.axis_index("path") * owned
    totals, moments = lax.psum((totals, moments), "path")
    point_value = totals / inner_total
    point_grad_all = moments / (inner_total * vol[:, None] * outer_state * jnp.sqrt(tau)[None, :])
    driver = driver_of(point_value)
    root_value = jnp.sum(totals) / (points * inner_total) + jnp.sum(driver) / points
    terminal = jnp.sum(
        jnp.sqrt(times)[None, :] * outer * totals[None, :] + jnp.sqrt(tau)[None, :] * moments,
        axis=1,
    )
    integral = jnp.sum(driver[None, :] * outer / jnp.sqrt(times)[None, :], axis=1)
    root_grad = terminal / (points * inner_total * vol * start) + integral / (points * vol * start)
    own_value = lax.dynamic_slice_in_dim(point_value, start_index, owned, 0)
    own_grad = lax.dynamic_slice_in_dim(point_grad_all, start_index, owned, 1)
    return (jnp.reshape(root_value, (1,)), root_grad, own_value, own_grad)


def row_tiles(rows):
    return [(r, min(16, rows - r)) for r in range(0, rows, 16)]


def as_columns(row, rows):
    full = -(-rows // LANES) * LANES
    row = jnp.concatenate([row, jnp.ones((1, full - rows), F32)], axis=1)
    return jnp.transpose(jnp.broadcast_to(row, (8, full)))[:, 0:1]


def swap_halves(block):
    return pltpu.roll(block, HALF, 1)


def low_lanes(shape):
    return lax.broadcasted_iota(jnp.int32, shape, 1) < HALF


def pack_low(top, bottom):
    return jnp.where(low_lanes(top.shape), top, swap_halves(bottom))


def pack_high(top, bottom):
    return jnp.where(low_lanes(top.shape), swap_halves(top), bottom)


def minima_kernel(
    noise_hbm, outer_hbm, start_hbm, vol_hbm, times_hbm, out_ref, noise_v,
    outer_ref, start_ref, vol_ref, times_ref, vol_s, level_v, sems,
):
    rows, paths, points = noise_hbm.shape
    cuts = [rows * c // CHUNKS // 16 * 16 for c in range(CHUNKS)] + [rows]
    spans = list(zip(cuts[:-1], cuts[1:]))
    copies = [
        pltpu.make_async_copy(noise_hbm.at[lo:hi], noise_v.at[lo:hi], sems.at[c])
        for c, (lo, hi) in enumerate(spans)
    ]
    small = [
        pltpu.make_async_copy(src, dst, sems.at[CHUNKS + c])
        for c, (src, dst) in enumerate(
            [
                (vol_hbm, vol_ref),
                (start_hbm, start_ref),
                (times_hbm, times_ref),
                (vol_hbm, vol_s),
                (outer_hbm, outer_ref),
            ]
        )
    ]
    for c in small + copies:
        c.start()
    for c in small[:4]:
        c.wait()
    vol_row = vol_ref[...]
    base = as_columns(jnp.log(start_ref[...]) + (drift - 0.5 * vol_row * vol_row), rows)
    vol = as_columns(vol_row, rows)
    times = times_ref[...]
    root_tau = jnp.sqrt(1.0 - times)
    inverse = 1.0 / root_tau
    ratio = jnp.sqrt(times) * inverse
    small[4].wait()
    for r, n in row_tiles(rows):
        drifted = base[r : r + n] * inverse
        level_v[r : r + n, :] = drifted + (vol[r : r + n] * ratio) * outer_ref[r : r + n, :].astype(F32)

    def level(d):
        return level_v[pl.ds(d, 1), :] + vol_s[0, d] * noise_v[d].astype(F32)

    low = jnp.full((paths, points), jnp.inf, F32)
    for (lo, hi), c in zip(spans, copies):
        c.wait()
        size = hi - lo
        whole = size // STEP

        def body(t, low, lo=lo):
            for j in range(STEP):
                low = jnp.minimum(low, level(lo + t * STEP + j))
            return low

        low = lax.fori_loop(0, whole, body, low)
        for d in range(lo + whole * STEP, hi):
            low = jnp.minimum(low, level(d))
    out_ref[...] = low * root_tau


def split(value):
    parts = []
    for _ in range(3):
        part = value.astype(jnp.bfloat16)
        value = value - part.astype(F32)
        parts.append(part)
    return parts


def owner(z, step, zs):
    half = zs // 2
    if step < half:
        return z ^ step
    turn = step - half
    up, down = half + (z + turn) % half, (z - half + turn + 1) % half
    if isinstance(z, int):
        return up if z < half else down
    return jnp.where(z < half, up, down)


def parts_kernel(zs, noise_ref, out_ref):
    paths, rows, points = noise_ref.shape
    me = lax.axis_index("path")
    z, y = me // 2, me % 2
    for s in range(zs):
        columns = pl.ds(pl.multiple_of(owner(z, s, zs) * LANES, LANES), LANES)

        def tile(k, r):
            n = min(16, rows - r)
            if n <= 0:
                return jnp.zeros((16, LANES), F32)
            part = noise_ref[k, r : r + n, columns].astype(F32)
            if n < 16:
                part = jnp.concatenate([part, jnp.zeros((16 - n, LANES), F32)], axis=0)
            return part

        for k in range(paths):
            for r in range(0, LANES, 16):
                top, bottom = tile(k, r), tile(k, LANES + r)
                out_ref[k, 2 * s + y, r : r + 16, :] = pack_low(top, bottom)
                out_ref[k, 2 * s + 1 - y, r : r + 16, :] = pack_high(top, bottom)


def moments_kernel(zs, n_lows, *refs):
    half = zs // 2
    lows, (parts_ref, times_ref, *rest) = refs[:n_lows], refs[n_lows:]
    send_far, keep_far, keep_near = rest[:3]
    send_near = rest[3 : 2 + half]
    pay, term = rest[2 + half :]
    paths, points = lows[0].shape
    me = lax.axis_index("path")
    z = me // 2
    first = me % 2 == 0
    payoff = jnp.exp(functools.reduce(jnp.minimum, [low[...] for low in lows]))
    pay[...] = payoff
    totals = jnp.sum(payoff, axis=0, keepdims=True)
    for s in range(zs):
        columns = pl.ds(pl.multiple_of(owner(z, s, zs) * LANES, LANES), LANES)
        both = jnp.concatenate([pay[:, columns], jnp.sqrt(1.0 - times_ref[0:1, columns])], axis=0)
        low, high = pack_low(both, both), pack_high(both, both)
        if s >= half:
            at = past = (s - half) * LANES
            same, other = keep_far, send_far
        else:
            at, past = 0, LANES
            same = other = keep_near if s == 0 else send_near[s - 1]
        for side, (ref, place) in enumerate(((same, at), (other, past))):
            rows = jnp.where(first, low, high) if side == 0 else jnp.where(first, high, low)
            weights = [jnp.broadcast_to(rows[k : k + 1], (8, LANES)) for k in range(paths + 1)]
            for r in range(0, LANES, 8):
                total = weights[0] * parts_ref[0, 2 * s + side, r : r + 8, :]
                for k in range(1, paths):
                    total = total + weights[k] * parts_ref[k, 2 * s + side, r : r + 8, :]
                ref[place + r : place + r + 8, :] = total
                if s == 0 and side == 0:
                    term[r : r + 8, :] = weights[paths] * total
                else:
                    term[r : r + 8, :] += weights[paths] * total
    extras = [totals[:, c : c + LANES] for c in range(0, points, LANES)]
    lanes_of = lax.broadcasted_iota(jnp.int32, (16, LANES), 1) // HALF
    picks = (lax.broadcasted_iota(jnp.int32, (16, LANES), 0) == lanes_of).astype(F32).astype(jnp.bfloat16)
    sums = sum(
        lax.dot_general(picks, part, (((1,), (1,)), ((), ())), preferred_element_type=F32)
        for part in split(term[...])
    )
    extras.append(sums[0 : EXTRA - len(extras), :])
    extras = jnp.concatenate(extras, axis=0)
    for ref in (send_far, keep_far, *send_near):
        ref[ref.shape[0] - EXTRA :, :] = extras
    keep_near[2 * LANES :, :] = jnp.zeros((EXTRA, LANES), F32)


def join_kernel(keep_ref, got_ref, *messages):
    tail = keep_ref.shape[0] - EXTRA
    extras = keep_ref[tail:, :] + got_ref[tail:, :]
    for n, ref in enumerate(messages):
        block = slice(n * LANES, (n + 1) * LANES)
        ref[0:LANES, :] = keep_ref[block, :] + got_ref[block, :]
        ref[LANES:, :] = extras


def scale_kernel(inner_total, outer_ref, start_ref, vol_ref, times_ref, out_ref):
    rows = outer_ref.shape[0]
    me = lax.axis_index("path")
    z = me // 2
    first = me % 2 == 0
    columns = pl.ds(pl.multiple_of(z * LANES, LANES), LANES)

    def pack(top, bottom):
        return jnp.where(first, pack_low(top, bottom), pack_high(top, bottom))

    vol = as_columns(vol_ref[...], rows)
    start = as_columns(start_ref[...], rows)
    spare = jnp.zeros((2 * LANES - rows, LANES), F32)
    outer = outer_ref[:, columns].astype(F32)
    outer = pack(outer[0:LANES], jnp.concatenate([outer[LANES:rows], spare], axis=0))
    times = times_ref[0:1, columns]
    times = pack(times, times)
    side = low_lanes((LANES, LANES))
    vol = jnp.where(side, vol[0:LANES], vol[LANES:])
    start = jnp.where(side, start[0:LANES], start[LANES:])
    state = start * jnp.exp((drift - 0.5 * vol * vol) * times + vol * jnp.sqrt(times) * outer)
    out_ref[...] = 1.0 / (inner_total * vol * state * jnp.sqrt(1.0 - times))


def final_kernel(
    inner_total, n_parts, near_ref, far_extra_ref, scale_ref, outer_ref, start_ref, vol_ref, times_ref, *rest
):
    parts, (value_ref, grad_ref, point_ref, point_grad_ref) = rest[:n_parts], rest[n_parts:]
    rows, points = outer_ref.shape
    me = lax.axis_index("path")
    first = me % 2 == 0
    moments = near_ref[0:LANES, :]
    extra = far_extra_ref[...] + near_ref[2 * LANES : 2 * LANES + EXTRA, :]
    for part in parts:
        moments = moments + part[0:LANES, :]
        extra = extra + part[LANES : LANES + EXTRA, :]
    grad = moments * scale_ref[...]
    turned = jnp.transpose(grad)
    point_grad_ref[:, 0:LANES] = turned[0:HALF]
    point_grad_ref[:, LANES:rows] = turned[HALF:, 0 : rows - LANES]
    blocks = points // LANES
    totals = jnp.concatenate([extra[c : c + 1, :] for c in range(blocks)], axis=1)
    inner_term = jnp.concatenate([extra[blocks : blocks + 1, :], extra[blocks + 1 : blocks + 2, :]], axis=1)
    values = totals * (1.0 / inner_total)
    driver = driver_of(values)
    value_ref[...] = jnp.sum(totals, axis=1, keepdims=True) * (1.0 / (points * inner_total)) + (
        jnp.sum(driver, axis=1, keepdims=True) * (1.0 / points)
    )
    own = extra[0:1, :]
    for c in range(1, blocks):
        own = jnp.where(me // 2 == c, extra[c : c + 1, :], own)
    own = jnp.where(first, own, swap_halves(own)) * (1.0 / inner_total)
    point_ref[...] = own[:, 0:HALF]
    root_times = jnp.sqrt(times_ref[...])
    weight = values * root_times + driver * (1.0 / root_times)
    parts_of = [part.astype(F32) for part in split(weight)]
    weights = jnp.concatenate(parts_of + [jnp.zeros((13, points), F32)], axis=0).astype(jnp.bfloat16)
    outer_term = jnp.sum(
        lax.dot_general(
            weights, outer_ref[...], (((1,), (1,)), ((), ())), preferred_element_type=F32
        ),
        axis=0,
        keepdims=True,
    )
    factor = 1.0 / (points * vol_ref[...] * start_ref[...])
    grad_ref[...] = (inner_term[:, 0:rows] * (1.0 / inner_total) + outer_term) * factor


def paired(inner_noise, outer_noise, start, vol, times):
    paths, rows, points = inner_noise.shape
    groups, dims = lax.axis_size("path"), lax.axis_size("dim")
    inner_total = paths * groups
    zs = groups // 2
    half = zs // 2
    start_row, vol_row, times_row = start[None, :], vol[None, :], times[None, :]
    limit = pltpu.CompilerParams(vmem_limit_bytes=16 * 1024 * 1024)

    lows, held_noise = pl.pallas_call(
        minima_kernel,
        out_shape=(
            pltpu.VMEM((paths, points), F32),
            pltpu.VMEM((rows, paths, points), inner_noise.dtype),
        ),
        in_specs=[pl.BlockSpec(memory_space=pltpu.HBM)] * 5,
        scratch_shapes=[
            pltpu.VMEM((rows, points), outer_noise.dtype),
            pltpu.VMEM((1, rows), F32),
            pltpu.VMEM((1, rows), F32),
            pltpu.VMEM((1, points), F32),
            pltpu.SMEM((1, rows), F32),
            pltpu.VMEM((rows, points), F32),
            pltpu.SemaphoreType.DMA((CHUNKS + 5,)),
        ],
        compiler_params=limit,
        name="minima",
    )(*[
        pltpu.with_memory_space_constraint(x, pltpu.HBM)
        for x in (jnp.transpose(inner_noise, (1, 0, 2)), outer_noise, start_row, vol_row, times_row)
    ])
    held_noise = jnp.transpose(held_noise, (1, 0, 2))

    others = [
        lax.ppermute(lows, "dim", [(i, i ^ s) for i in range(dims)])
        for s in sorted(range(1, dims), key=lambda s: (s < 2, s))
    ]

    parts = pl.pallas_call(
        functools.partial(parts_kernel, zs),
        out_shape=pltpu.VMEM((paths, 2 * zs, LANES, LANES), F32),
        compiler_params=limit,
        cost_estimate=pl.CostEstimate(
            flops=paths * rows * points, bytes_accessed=6 * paths * rows * points, transcendentals=0
        ),
        name="parts",
    )(held_noise)

    send_far, keep_far, keep_near, *send_near = pl.pallas_call(
        functools.partial(moments_kernel, zs, dims),
        out_shape=[pltpu.VMEM((half * LANES + EXTRA, LANES), F32)] * 2
        + [pltpu.VMEM((2 * LANES + EXTRA, LANES), F32)] * half,
        scratch_shapes=[pltpu.VMEM((paths, points), F32), pltpu.VMEM((LANES, LANES), F32)],
        compiler_params=limit,
        name="moments",
    )(lows, *others, parts, times_row)

    def along_z(message, step):
        route = [(i, 2 * owner(i // 2, step, zs) + i % 2) for i in range(groups)]
        return lax.ppermute(message, "path", route)

    def along_y(message):
        return lax.ppermute(message, "path", [(i, i ^ 1) for i in range(groups)])

    messages = pl.pallas_call(
        join_kernel,
        out_shape=[pltpu.VMEM((LANES + EXTRA, LANES), F32)] * half,
        compiler_params=limit,
        name="join",
    )(keep_far, along_y(send_far))
    near_sum = keep_near
    for step in range(1, half):
        near_sum = near_sum + along_z(send_near[step - 1], step)
    scale = pl.pallas_call(
        functools.partial(scale_kernel, inner_total),
        out_shape=pltpu.VMEM((LANES, LANES), F32),
        compiler_params=limit,
        name="scale",
    )(outer_noise, start_row, vol_row, times_row)
    far_extra = messages[0][LANES:]
    arrived = [along_z(message, half + n) for n, message in enumerate(messages)]
    arrived.append(along_y(near_sum[LANES:]))

    value, grad, point, point_grad = pl.pallas_call(
        functools.partial(final_kernel, inner_total, len(arrived)),
        out_shape=[
            jax.ShapeDtypeStruct((1, 1), F32),
            jax.ShapeDtypeStruct((1, rows), F32),
            jax.ShapeDtypeStruct((1, points // groups), F32),
            jax.ShapeDtypeStruct((points // groups, rows), F32),
        ],
        compiler_params=limit,
        name="final",
    )(near_sum, far_extra, scale, outer_noise, start_row, vol_row, times_row, *arrived)
    return value.reshape(1), grad.reshape(rows), point.reshape(points // groups), jnp.transpose(point_grad)


def per_device(inner_noise, outer_noise, start, vol, times):
    rows, points = outer_noise.shape
    groups, dims = lax.axis_size("path"), lax.axis_size("dim")
    fits = (
        2 * points == LANES * groups
        and LANES < rows <= 2 * LANES
        and is_power(groups)
        and groups >= 4
        and is_power(dims)
        and dims > 1
        and points // LANES + 2 <= EXTRA
    )
    return (paired if fits else general)(inner_noise, outer_noise, start, vol, times)


def solution(mesh):
    in_specs = (P("path", "dim", None), P("dim", None), P("dim"), P("dim"), P())
    out_specs = (P(), P("dim"), P("path"), P("dim", "path"))
    return jax.shard_map(
        per_device, mesh=mesh, in_specs=in_specs, out_specs=out_specs, check_vma=False
    )
```

```python
import functools

import jax
import jax.numpy as jnp
from jax import lax
from jax.experimental import pallas as pl
from jax.experimental.pallas import tpu as pltpu
from jax.sharding import PartitionSpec as P

drift = 0.02
delta = 2.0 / 3.0
rate_free = 0.02
gamma_high = 0.2
gamma_low = 0.02
value_high = 0.4
value_low = 0.7

LANES = 128
HALF = LANES // 2
EXTRA = 8
CHUNKS = 6
STEP = 16
F32 = jnp.float32


def driver_of(value):
    slope = jnp.clip((value - value_high) / (value_low - value_high), 0.0, 1.0)
    quota = gamma_high + (gamma_low - gamma_high) * slope
    return -(1.0 - delta) * quota * value - rate_free * value


def is_power(n):
    return n > 0 and n & (n - 1) == 0


def general(inner_noise, outer_noise, start, vol, times):
    paths_here = inner_noise.shape[0]
    points = times.shape[0]
    groups = lax.axis_size("path")
    inner_total = paths_here * groups
    owned = points // groups
    tau = 1.0 - times
    outer = outer_noise.astype(F32)
    mean_rate = (drift - 0.5 * vol * vol)[:, None]
    outer_state = start[:, None] * jnp.exp(
        mean_rate * times[None, :] + vol[:, None] * jnp.sqrt(times)[None, :] * outer
    )
    shock = inner_noise.astype(F32)
    level = outer_state[None] * jnp.exp(
        (mean_rate * tau[None, :])[None] + (vol[:, None] * jnp.sqrt(tau)[None, :])[None] * shock
    )
    payoff = lax.pmin(jnp.min(level, axis=1), "dim")
    totals = jnp.sum(payoff, axis=0)
    moments = jnp.sum(payoff[:, None, :] * shock, axis=0)
    start_index = lax.axis_index("path") * owned
    totals, moments = lax.psum((totals, moments), "path")
    point_value = totals / inner_total
    point_grad_all = moments / (inner_total * vol[:, None] * outer_state * jnp.sqrt(tau)[None, :])
    driver = driver_of(point_value)
    root_value = jnp.sum(totals) / (points * inner_total) + jnp.sum(driver) / points
    terminal = jnp.sum(
        jnp.sqrt(times)[None, :] * outer * totals[None, :] + jnp.sqrt(tau)[None, :] * moments,
        axis=1,
    )
    integral = jnp.sum(driver[None, :] * outer / jnp.sqrt(times)[None, :], axis=1)
    root_grad = terminal / (points * inner_total * vol * start) + integral / (points * vol * start)
    own_value = lax.dynamic_slice_in_dim(point_value, start_index, owned, 0)
    own_grad = lax.dynamic_slice_in_dim(point_grad_all, start_index, owned, 1)
    return (jnp.reshape(root_value, (1,)), root_grad, own_value, own_grad)


def row_tiles(rows):
    return [(r, min(16, rows - r)) for r in range(0, rows, 16)]


def as_columns(row, rows):
    full = -(-rows // LANES) * LANES
    row = jnp.concatenate([row, jnp.ones((1, full - rows), F32)], axis=1)
    return jnp.transpose(jnp.broadcast_to(row, (8, full)))[:, 0:1]


def swap_halves(block):
    return pltpu.roll(block, HALF, 1)


def low_lanes(shape):
    return lax.broadcasted_iota(jnp.int32, shape, 1) < HALF


def pack_low(top, bottom):
    return jnp.where(low_lanes(top.shape), top, swap_halves(bottom))


def pack_high(top, bottom):
    return jnp.where(low_lanes(top.shape), swap_halves(top), bottom)


def minima_kernel(
    noise_hbm, outer_hbm, start_hbm, vol_hbm, times_hbm, out_ref, noise_v,
    outer_ref, start_ref, vol_ref, times_ref, vol_s, level_v, sems,
):
    rows, paths, points = noise_hbm.shape
    cuts = [rows * c // CHUNKS // 16 * 16 for c in range(CHUNKS)] + [rows]
    spans = list(zip(cuts[:-1], cuts[1:]))
    copies = [
        pltpu.make_async_copy(noise_hbm.at[lo:hi], noise_v.at[lo:hi], sems.at[c])
        for c, (lo, hi) in enumerate(spans)
    ]
    small = [
        pltpu.make_async_copy(src, dst, sems.at[CHUNKS + c])
        for c, (src, dst) in enumerate(
            [
                (vol_hbm, vol_ref),
                (start_hbm, start_ref),
                (times_hbm, times_ref),
                (vol_hbm, vol_s),
                (outer_hbm, outer_ref),
            ]
        )
    ]
    for c in small + copies:
        c.start()
    for c in small[:4]:
        c.wait()
    vol_row = vol_ref[...]
    base = as_columns(jnp.log(start_ref[...]) + (drift - 0.5 * vol_row * vol_row), rows)
    vol = as_columns(vol_row, rows)
    times = times_ref[...]
    root_tau = jnp.sqrt(1.0 - times)
    inverse = 1.0 / root_tau
    ratio = jnp.sqrt(times) * inverse
    small[4].wait()
    for r, n in row_tiles(rows):
        drifted = base[r : r + n] * inverse
        level_v[r : r + n, :] = drifted + (vol[r : r + n] * ratio) * outer_ref[r : r + n, :].astype(F32)

    def level(d):
        return level_v[pl.ds(d, 1), :] + vol_s[0, d] * noise_v[d].astype(F32)

    low = jnp.full((paths, points), jnp.inf, F32)
    for (lo, hi), c in zip(spans, copies):
        c.wait()
        size = hi - lo
        whole = size // STEP

        def body(t, low, lo=lo):
            for j in range(STEP):
                low = jnp.minimum(low, level(lo + t * STEP + j))
            return low

        low = lax.fori_loop(0, whole, body, low)
        for d in range(lo + whole * STEP, hi):
            low = jnp.minimum(low, level(d))
    out_ref[...] = low * root_tau


def split(value):
    parts = []
    for _ in range(3):
        part = value.astype(jnp.bfloat16)
        value = value - part.astype(F32)
        parts.append(part)
    return parts


def owner(z, step, zs):
    half = zs // 2
    if step < half:
        return z ^ step
    turn = step - half
    up, down = half + (z + turn) % half, (z - half + turn + 1) % half
    if isinstance(z, int):
        return up if z < half else down
    return jnp.where(z < half, up, down)


def parts_kernel(zs, noise_ref, out_ref):
    paths, rows, points = noise_ref.shape
    me = lax.axis_index("path")
    z, y = me // 2, me % 2
    for s in range(zs):
        columns = pl.ds(pl.multiple_of(owner(z, s, zs) * LANES, LANES), LANES)

        def tile(k, r):
            n = min(16, rows - r)
            if n <= 0:
                return jnp.zeros((16, LANES), F32)
            part = noise_ref[k, r : r + n, columns].astype(F32)
            if n < 16:
                part = jnp.concatenate([part, jnp.zeros((16 - n, LANES), F32)], axis=0)
            return part

        for k in range(paths):
            for r in range(0, LANES, 16):
                top, bottom = tile(k, r), tile(k, LANES + r)
                out_ref[k, 2 * s + y, r : r + 16, :] = pack_low(top, bottom)
                out_ref[k, 2 * s + 1 - y, r : r + 16, :] = pack_high(top, bottom)


def moments_kernel(zs, n_lows, *refs):
    half = zs // 2
    lows, (parts_ref, times_ref, *rest) = refs[:n_lows], refs[n_lows:]
    send_far, keep_far, keep_near = rest[:3]
    send_near = rest[3 : 2 + half]
    pay, term = rest[2 + half :]
    paths, points = lows[0].shape
    me = lax.axis_index("path")
    z = me // 2
    first = me % 2 == 0
    payoff = jnp.exp(functools.reduce(jnp.minimum, [low[...] for low in lows]))
    pay[...] = payoff
    totals = jnp.sum(payoff, axis=0, keepdims=True)
    for s in range(zs):
        columns = pl.ds(pl.multiple_of(owner(z, s, zs) * LANES, LANES), LANES)
        both = jnp.concatenate([pay[:, columns], jnp.sqrt(1.0 - times_ref[0:1, columns])], axis=0)
        low, high = pack_low(both, both), pack_high(both, both)
        if s >= half:
            at = past = (s - half) * LANES
            same, other = keep_far, send_far
        else:
            at, past = 0, LANES
            same = other = keep_near if s == 0 else send_near[s - 1]
        for side, (ref, place) in enumerate(((same, at), (other, past))):
            rows = jnp.where(first, low, high) if side == 0 else jnp.where(first, high, low)
            weights = [jnp.broadcast_to(rows[k : k + 1], (8, LANES)) for k in range(paths + 1)]
            for r in range(0, LANES, 8):
                total = weights[0] * parts_ref[0, 2 * s + side, r : r + 8, :]
                for k in range(1, paths):
                    total = total + weights[k] * parts_ref[k, 2 * s + side, r : r + 8, :]
                ref[place + r : place + r + 8, :] = total
                if s == 0 and side == 0:
                    term[r : r + 8, :] = weights[paths] * total
                else:
                    term[r : r + 8, :] += weights[paths] * total
    extras = [totals[:, c : c + LANES] for c in range(0, points, LANES)]
    lanes_of = lax.broadcasted_iota(jnp.int32, (16, LANES), 1) // HALF
    picks = (lax.broadcasted_iota(jnp.int32, (16, LANES), 0) == lanes_of).astype(F32).astype(jnp.bfloat16)
    sums = sum(
        lax.dot_general(picks, part, (((1,), (1,)), ((), ())), preferred_element_type=F32)
        for part in split(term[...])
    )
    extras.append(sums[0 : EXTRA - len(extras), :])
    extras = jnp.concatenate(extras, axis=0)
    for ref in (send_far, keep_far, *send_near):
        ref[ref.shape[0] - EXTRA :, :] = extras
    keep_near[2 * LANES :, :] = jnp.zeros((EXTRA, LANES), F32)


def join_kernel(keep_ref, got_ref, *messages):
    tail = keep_ref.shape[0] - EXTRA
    extras = keep_ref[tail:, :] + got_ref[tail:, :]
    for n, ref in enumerate(messages):
        block = slice(n * LANES, (n + 1) * LANES)
        ref[0:LANES, :] = keep_ref[block, :] + got_ref[block, :]
        ref[LANES:, :] = extras


def scale_kernel(inner_total, outer_ref, start_ref, vol_ref, times_ref, out_ref):
    rows = outer_ref.shape[0]
    me = lax.axis_index("path")
    z = me // 2
    first = me % 2 == 0
    columns = pl.ds(pl.multiple_of(z * LANES, LANES), LANES)

    def pack(top, bottom):
        return jnp.where(first, pack_low(top, bottom), pack_high(top, bottom))

    vol = as_columns(vol_ref[...], rows)
    start = as_columns(start_ref[...], rows)
    spare = jnp.zeros((2 * LANES - rows, LANES), F32)
    outer = outer_ref[:, columns].astype(F32)
    outer = pack(outer[0:LANES], jnp.concatenate([outer[LANES:rows], spare], axis=0))
    times = times_ref[0:1, columns]
    times = pack(times, times)
    side = low_lanes((LANES, LANES))
    vol = jnp.where(side, vol[0:LANES], vol[LANES:])
    start = jnp.where(side, start[0:LANES], start[LANES:])
    state = start * jnp.exp((drift - 0.5 * vol * vol) * times + vol * jnp.sqrt(times) * outer)
    out_ref[...] = 1.0 / (inner_total * vol * state * jnp.sqrt(1.0 - times))


def final_kernel(
    inner_total, n_parts, near_ref, far_extra_ref, scale_ref, outer_ref, start_ref, vol_ref, times_ref, *rest
):
    parts, (value_ref, grad_ref, point_ref, point_grad_ref) = rest[:n_parts], rest[n_parts:]
    rows, points = outer_ref.shape
    me = lax.axis_index("path")
    first = me % 2 == 0
    moments = near_ref[0:LANES, :]
    extra = far_extra_ref[...] + near_ref[2 * LANES : 2 * LANES + EXTRA, :]
    for part in parts:
        moments = moments + part[0:LANES, :]
        extra = extra + part[LANES : LANES + EXTRA, :]
    grad = moments * scale_ref[...]
    turned = jnp.transpose(grad)
    point_grad_ref[:, 0:LANES] = turned[0:HALF]
    point_grad_ref[:, LANES:rows] = turned[HALF:, 0 : rows - LANES]
    blocks = points // LANES
    totals = jnp.concatenate([extra[c : c + 1, :] for c in range(blocks)], axis=1)
    inner_term = jnp.concatenate([extra[blocks : blocks + 1, :], extra[blocks + 1 : blocks + 2, :]], axis=1)
    values = totals / inner_total
    driver = driver_of(values)
    value_ref[...] = jnp.sum(totals, axis=1, keepdims=True) / (points * inner_total) + (
        jnp.sum(driver, axis=1, keepdims=True) / points
    )
    own = extra[0:1, :]
    for c in range(1, blocks):
        own = jnp.where(me // 2 == c, extra[c : c + 1, :], own)
    own = jnp.where(first, own, swap_halves(own)) / inner_total
    point_ref[...] = own[:, 0:HALF]
    root_times = jnp.sqrt(times_ref[...])
    weight = totals * root_times / inner_total + driver / root_times
    parts_of = [part.astype(F32) for part in split(weight)]
    weights = jnp.concatenate(parts_of + [jnp.zeros((13, points), F32)], axis=0).astype(jnp.bfloat16)
    outer_term = jnp.sum(
        lax.dot_general(
            weights, outer_ref[...], (((1,), (1,)), ((), ())), preferred_element_type=F32
        ),
        axis=0,
        keepdims=True,
    )
    grad_ref[...] = (inner_term[:, 0:rows] / inner_total + outer_term) / (
        points * vol_ref[...] * start_ref[...]
    )


def paired(inner_noise, outer_noise, start, vol, times):
    paths, rows, points = inner_noise.shape
    groups, dims = lax.axis_size("path"), lax.axis_size("dim")
    inner_total = paths * groups
    zs = groups // 2
    half = zs // 2
    start_row, vol_row, times_row = start[None, :], vol[None, :], times[None, :]
    limit = pltpu.CompilerParams(vmem_limit_bytes=16 * 1024 * 1024)

    lows, held_noise = pl.pallas_call(
        minima_kernel,
        out_shape=(
            pltpu.VMEM((paths, points), F32),
            pltpu.VMEM((rows, paths, points), inner_noise.dtype),
        ),
        in_specs=[pl.BlockSpec(memory_space=pltpu.HBM)] * 5,
        scratch_shapes=[
            pltpu.VMEM((rows, points), outer_noise.dtype),
            pltpu.VMEM((1, rows), F32),
            pltpu.VMEM((1, rows), F32),
            pltpu.VMEM((1, points), F32),
            pltpu.SMEM((1, rows), F32),
            pltpu.VMEM((rows, points), F32),
            pltpu.SemaphoreType.DMA((CHUNKS + 5,)),
        ],
        compiler_params=limit,
        name="minima",
    )(*[
        pltpu.with_memory_space_constraint(x, pltpu.HBM)
        for x in (jnp.transpose(inner_noise, (1, 0, 2)), outer_noise, start_row, vol_row, times_row)
    ])
    held_noise = jnp.transpose(held_noise, (1, 0, 2))

    others = [
        lax.ppermute(lows, "dim", [(i, i ^ s) for i in range(dims)])
        for s in sorted(range(1, dims), key=lambda s: (s < 2, s))
    ]

    parts = pl.pallas_call(
        functools.partial(parts_kernel, zs),
        out_shape=pltpu.VMEM((paths, 2 * zs, LANES, LANES), F32),
        compiler_params=limit,
        cost_estimate=pl.CostEstimate(
            flops=paths * rows * points, bytes_accessed=6 * paths * rows * points, transcendentals=0
        ),
        name="parts",
    )(held_noise)

    send_far, keep_far, keep_near, *send_near = pl.pallas_call(
        functools.partial(moments_kernel, zs, dims),
        out_shape=[pltpu.VMEM((half * LANES + EXTRA, LANES), F32)] * 2
        + [pltpu.VMEM((2 * LANES + EXTRA, LANES), F32)] * half,
        scratch_shapes=[pltpu.VMEM((paths, points), F32), pltpu.VMEM((LANES, LANES), F32)],
        compiler_params=limit,
        name="moments",
    )(lows, *others, parts, times_row)

    def along_z(message, step):
        route = [(i, 2 * owner(i // 2, step, zs) + i % 2) for i in range(groups)]
        return lax.ppermute(message, "path", route)

    def along_y(message):
        return lax.ppermute(message, "path", [(i, i ^ 1) for i in range(groups)])

    messages = pl.pallas_call(
        join_kernel,
        out_shape=[pltpu.VMEM((LANES + EXTRA, LANES), F32)] * half,
        compiler_params=limit,
        name="join",
    )(keep_far, along_y(send_far))
    near_sum = keep_near
    for step in range(1, half):
        near_sum = near_sum + along_z(send_near[step - 1], step)
    scale = pl.pallas_call(
        functools.partial(scale_kernel, inner_total),
        out_shape=pltpu.VMEM((LANES, LANES), F32),
        compiler_params=limit,
        name="scale",
    )(outer_noise, start_row, vol_row, times_row)
    far_extra = messages[0][LANES:]
    arrived = [along_z(message, half + n) for n, message in enumerate(messages)]
    arrived.append(along_y(near_sum[LANES:]))

    value, grad, point, point_grad = pl.pallas_call(
        functools.partial(final_kernel, inner_total, len(arrived)),
        out_shape=[
            jax.ShapeDtypeStruct((1, 1), F32),
            jax.ShapeDtypeStruct((1, rows), F32),
            jax.ShapeDtypeStruct((1, points // groups), F32),
            jax.ShapeDtypeStruct((points // groups, rows), F32),
        ],
        compiler_params=limit,
        name="final",
    )(near_sum, far_extra, scale, outer_noise, start_row, vol_row, times_row, *arrived)
    return value.reshape(1), grad.reshape(rows), point.reshape(points // groups), jnp.transpose(point_grad)


def per_device(inner_noise, outer_noise, start, vol, times):
    rows, points = outer_noise.shape
    groups, dims = lax.axis_size("path"), lax.axis_size("dim")
    fits = (
        2 * points == LANES * groups
        and LANES < rows <= 2 * LANES
        and is_power(groups)
        and groups >= 4
        and is_power(dims)
        and dims > 1
        and points // LANES + 2 <= EXTRA
    )
    return (paired if fits else general)(inner_noise, outer_noise, start, vol, times)


def solution(mesh):
    in_specs = (P("path", "dim", None), P("dim", None), P("dim"), P("dim"), P())
    out_specs = (P(), P("dim"), P("path"), P("dim", "path"))
    return jax.shard_map(
        per_device, mesh=mesh, in_specs=in_specs, out_specs=out_specs, check_vma=False
    )
```

```python
import functools

import jax
import jax.numpy as jnp
from jax import lax
from jax.experimental import pallas as pl
from jax.experimental.pallas import tpu as pltpu
from jax.sharding import PartitionSpec as P

drift = 0.02
delta = 2.0 / 3.0
rate_free = 0.02
gamma_high = 0.2
gamma_low = 0.02
value_high = 0.4
value_low = 0.7

LANES = 128
HALF = LANES // 2
EXTRA = 8
CHUNKS = 6
STEP = 16
F32 = jnp.float32


def driver_of(value):
    slope = jnp.clip((value - value_high) * (1.0 / (value_low - value_high)), 0.0, 1.0)
    quota = gamma_high + (gamma_low - gamma_high) * slope
    return -(1.0 - delta) * quota * value - rate_free * value


def is_power(n):
    return n > 0 and n & (n - 1) == 0


def general(inner_noise, outer_noise, start, vol, times):
    paths_here = inner_noise.shape[0]
    points = times.shape[0]
    groups = lax.axis_size("path")
    inner_total = paths_here * groups
    owned = points // groups
    tau = 1.0 - times
    outer = outer_noise.astype(F32)
    mean_rate = (drift - 0.5 * vol * vol)[:, None]
    outer_state = start[:, None] * jnp.exp(
        mean_rate * times[None, :] + vol[:, None] * jnp.sqrt(times)[None, :] * outer
    )
    shock = inner_noise.astype(F32)
    level = outer_state[None] * jnp.exp(
        (mean_rate * tau[None, :])[None] + (vol[:, None] * jnp.sqrt(tau)[None, :])[None] * shock
    )
    payoff = lax.pmin(jnp.min(level, axis=1), "dim")
    totals = jnp.sum(payoff, axis=0)
    moments = jnp.sum(payoff[:, None, :] * shock, axis=0)
    start_index = lax.axis_index("path") * owned
    totals, moments = lax.psum((totals, moments), "path")
    point_value = totals / inner_total
    point_grad_all = moments / (inner_total * vol[:, None] * outer_state * jnp.sqrt(tau)[None, :])
    driver = driver_of(point_value)
    root_value = jnp.sum(totals) / (points * inner_total) + jnp.sum(driver) / points
    terminal = jnp.sum(
        jnp.sqrt(times)[None, :] * outer * totals[None, :] + jnp.sqrt(tau)[None, :] * moments,
        axis=1,
    )
    integral = jnp.sum(driver[None, :] * outer / jnp.sqrt(times)[None, :], axis=1)
    root_grad = terminal / (points * inner_total * vol * start) + integral / (points * vol * start)
    own_value = lax.dynamic_slice_in_dim(point_value, start_index, owned, 0)
    own_grad = lax.dynamic_slice_in_dim(point_grad_all, start_index, owned, 1)
    return (jnp.reshape(root_value, (1,)), root_grad, own_value, own_grad)


def row_tiles(rows):
    return [(r, min(16, rows - r)) for r in range(0, rows, 16)]


def as_columns(row, rows):
    full = -(-rows // LANES) * LANES
    row = jnp.concatenate([row, jnp.ones((1, full - rows), F32)], axis=1)
    return jnp.transpose(jnp.broadcast_to(row, (8, full)))[:, 0:1]


def swap_halves(block):
    return pltpu.roll(block, HALF, 1)


def low_lanes(shape):
    return lax.broadcasted_iota(jnp.int32, shape, 1) < HALF


def pack_low(top, bottom):
    return jnp.where(low_lanes(top.shape), top, swap_halves(bottom))


def pack_high(top, bottom):
    return jnp.where(low_lanes(top.shape), swap_halves(top), bottom)


def minima_kernel(
    noise_hbm, outer_hbm, start_hbm, vol_hbm, times_hbm, out_ref, noise_v,
    outer_ref, start_ref, vol_ref, times_ref, vol_s, level_v, sems,
):
    rows, paths, points = noise_hbm.shape
    cuts = [rows * c // CHUNKS // 16 * 16 for c in range(CHUNKS)] + [rows]
    spans = list(zip(cuts[:-1], cuts[1:]))
    copies = [
        pltpu.make_async_copy(noise_hbm.at[lo:hi], noise_v.at[lo:hi], sems.at[c])
        for c, (lo, hi) in enumerate(spans)
    ]
    small = [
        pltpu.make_async_copy(src, dst, sems.at[CHUNKS + c])
        for c, (src, dst) in enumerate(
            [
                (vol_hbm, vol_ref),
                (start_hbm, start_ref),
                (times_hbm, times_ref),
                (vol_hbm, vol_s),
                (outer_hbm, outer_ref),
            ]
        )
    ]
    for c in small + copies:
        c.start()
    for c in small[:4]:
        c.wait()
    vol_row = vol_ref[...]
    base = as_columns(jnp.log(start_ref[...]) + (drift - 0.5 * vol_row * vol_row), rows)
    vol = as_columns(vol_row, rows)
    times = times_ref[...]
    root_tau = jnp.sqrt(1.0 - times)
    inverse = 1.0 / root_tau
    ratio = jnp.sqrt(times) * inverse
    small[4].wait()
    for r, n in row_tiles(rows):
        drifted = base[r : r + n] * inverse
        level_v[r : r + n, :] = drifted + (vol[r : r + n] * ratio) * outer_ref[r : r + n, :].astype(F32)

    def level(d):
        return level_v[pl.ds(d, 1), :] + vol_s[0, d] * noise_v[d].astype(F32)

    low = jnp.full((paths, points), jnp.inf, F32)
    for (lo, hi), c in zip(spans, copies):
        c.wait()
        size = hi - lo
        whole = size // STEP

        def body(t, low, lo=lo):
            for j in range(STEP):
                low = jnp.minimum(low, level(lo + t * STEP + j))
            return low

        low = lax.fori_loop(0, whole, body, low)
        for d in range(lo + whole * STEP, hi):
            low = jnp.minimum(low, level(d))
    out_ref[...] = low * root_tau


def split(value):
    parts = []
    for _ in range(3):
        part = value.astype(jnp.bfloat16)
        value = value - part.astype(F32)
        parts.append(part)
    return parts


def owner(z, step, zs):
    half = zs // 2
    if step < half:
        return z ^ step
    turn = step - half
    up, down = half + (z + turn) % half, (z - half + turn + 1) % half
    if isinstance(z, int):
        return up if z < half else down
    return jnp.where(z < half, up, down)


def parts_kernel(zs, noise_ref, out_ref):
    paths, rows, points = noise_ref.shape
    me = lax.axis_index("path")
    z, y = me // 2, me % 2
    for s in range(zs):
        columns = pl.ds(pl.multiple_of(owner(z, s, zs) * LANES, LANES), LANES)

        def tile(k, r):
            n = min(16, rows - r)
            if n <= 0:
                return jnp.zeros((16, LANES), F32)
            part = noise_ref[k, r : r + n, columns].astype(F32)
            if n < 16:
                part = jnp.concatenate([part, jnp.zeros((16 - n, LANES), F32)], axis=0)
            return part

        for k in range(paths):
            for r in range(0, LANES, 16):
                top, bottom = tile(k, r), tile(k, LANES + r)
                out_ref[k, 2 * s + y, r : r + 16, :] = pack_low(top, bottom)
                out_ref[k, 2 * s + 1 - y, r : r + 16, :] = pack_high(top, bottom)


def moments_kernel(zs, n_lows, *refs):
    half = zs // 2
    lows, (parts_ref, times_ref, *rest) = refs[:n_lows], refs[n_lows:]
    send_far, keep_far, keep_near = rest[:3]
    send_near = rest[3 : 2 + half]
    pay, term = rest[2 + half :]
    paths, points = lows[0].shape
    me = lax.axis_index("path")
    z = me // 2
    first = me % 2 == 0
    payoff = jnp.exp(functools.reduce(jnp.minimum, [low[...] for low in lows]))
    pay[...] = payoff
    totals = jnp.sum(payoff, axis=0, keepdims=True)
    for s in range(zs):
        columns = pl.ds(pl.multiple_of(owner(z, s, zs) * LANES, LANES), LANES)
        both = jnp.concatenate([pay[:, columns], jnp.sqrt(1.0 - times_ref[0:1, columns])], axis=0)
        low, high = pack_low(both, both), pack_high(both, both)
        if s >= half:
            at = past = (s - half) * LANES
            same, other = keep_far, send_far
        else:
            at, past = 0, LANES
            same = other = keep_near if s == 0 else send_near[s - 1]
        for side, (ref, place) in enumerate(((same, at), (other, past))):
            rows = jnp.where(first, low, high) if side == 0 else jnp.where(first, high, low)
            weights = [jnp.broadcast_to(rows[k : k + 1], (8, LANES)) for k in range(paths + 1)]
            for r in range(0, LANES, 8):
                total = weights[0] * parts_ref[0, 2 * s + side, r : r + 8, :]
                for k in range(1, paths):
                    total = total + weights[k] * parts_ref[k, 2 * s + side, r : r + 8, :]
                ref[place + r : place + r + 8, :] = total
                if s == 0 and side == 0:
                    term[r : r + 8, :] = weights[paths] * total
                else:
                    term[r : r + 8, :] += weights[paths] * total
    extras = [totals[:, c : c + LANES] for c in range(0, points, LANES)]
    lanes_of = lax.broadcasted_iota(jnp.int32, (16, LANES), 1) // HALF
    picks = (lax.broadcasted_iota(jnp.int32, (16, LANES), 0) == lanes_of).astype(F32).astype(jnp.bfloat16)
    sums = sum(
        lax.dot_general(picks, part, (((1,), (1,)), ((), ())), preferred_element_type=F32)
        for part in split(term[...])
    )
    extras.append(sums[0 : EXTRA - len(extras), :])
    extras = jnp.concatenate(extras, axis=0)
    for ref in (send_far, keep_far, *send_near):
        ref[ref.shape[0] - EXTRA :, :] = extras
    keep_near[2 * LANES :, :] = jnp.zeros((EXTRA, LANES), F32)


def join_kernel(keep_ref, got_ref, *messages):
    tail = keep_ref.shape[0] - EXTRA
    extras = keep_ref[tail:, :] + got_ref[tail:, :]
    for n, ref in enumerate(messages):
        block = slice(n * LANES, (n + 1) * LANES)
        ref[0:LANES, :] = keep_ref[block, :] + got_ref[block, :]
        ref[LANES:, :] = extras


def scale_kernel(inner_total, outer_ref, start_ref, vol_ref, times_ref, out_ref):
    rows = outer_ref.shape[0]
    me = lax.axis_index("path")
    z = me // 2
    first = me % 2 == 0
    columns = pl.ds(pl.multiple_of(z * LANES, LANES), LANES)

    def pack(top, bottom):
        return jnp.where(first, pack_low(top, bottom), pack_high(top, bottom))

    vol = as_columns(vol_ref[...], rows)
    start = as_columns(start_ref[...], rows)
    spare = jnp.zeros((2 * LANES - rows, LANES), F32)
    outer = outer_ref[:, columns].astype(F32)
    outer = pack(outer[0:LANES], jnp.concatenate([outer[LANES:rows], spare], axis=0))
    times = times_ref[0:1, columns]
    times = pack(times, times)
    side = low_lanes((LANES, LANES))
    vol = jnp.where(side, vol[0:LANES], vol[LANES:])
    start = jnp.where(side, start[0:LANES], start[LANES:])
    state = start * jnp.exp((drift - 0.5 * vol * vol) * times + vol * jnp.sqrt(times) * outer)
    out_ref[...] = 1.0 / (inner_total * vol * state * jnp.sqrt(1.0 - times))


def final_kernel(
    inner_total, n_parts, near_ref, far_extra_ref, scale_ref, outer_ref, start_ref, vol_ref, times_ref, *rest
):
    parts, (value_ref, grad_ref, point_ref, point_grad_ref) = rest[:n_parts], rest[n_parts:]
    rows, points = outer_ref.shape
    me = lax.axis_index("path")
    first = me % 2 == 0
    moments = near_ref[0:LANES, :]
    extra = far_extra_ref[...] + near_ref[2 * LANES : 2 * LANES + EXTRA, :]
    for part in parts:
        moments = moments + part[0:LANES, :]
        extra = extra + part[LANES : LANES + EXTRA, :]
    grad = moments * scale_ref[...]
    turned = jnp.transpose(grad)
    point_grad_ref[:, 0:LANES] = turned[0:HALF]
    point_grad_ref[:, LANES:rows] = turned[HALF:, 0 : rows - LANES]
    blocks = points // LANES
    totals = jnp.concatenate([extra[c : c + 1, :] for c in range(blocks)], axis=1)
    inner_term = jnp.concatenate([extra[blocks : blocks + 1, :], extra[blocks + 1 : blocks + 2, :]], axis=1)
    values = totals * (1.0 / inner_total)
    driver = driver_of(values)
    value_ref[...] = jnp.sum(totals, axis=1, keepdims=True) * (1.0 / (points * inner_total)) + (
        jnp.sum(driver, axis=1, keepdims=True) * (1.0 / points)
    )
    own = extra[0:1, :]
    for c in range(1, blocks):
        own = jnp.where(me // 2 == c, extra[c : c + 1, :], own)
    own = jnp.where(first, own, swap_halves(own)) * (1.0 / inner_total)
    point_ref[...] = own[:, 0:HALF]
    root_times = jnp.sqrt(times_ref[...])
    weight = values * root_times + driver * (1.0 / root_times)
    parts_of = [part.astype(F32) for part in split(weight)]
    weights = jnp.concatenate(parts_of + [jnp.zeros((13, points), F32)], axis=0).astype(jnp.bfloat16)
    outer_term = jnp.sum(
        lax.dot_general(
            weights, outer_ref[...], (((1,), (1,)), ((), ())), preferred_element_type=F32
        ),
        axis=0,
        keepdims=True,
    )
    factor = 1.0 / (points * vol_ref[...] * start_ref[...])
    grad_ref[...] = (inner_term[:, 0:rows] * (1.0 / inner_total) + outer_term) * factor


def paired(inner_noise, outer_noise, start, vol, times):
    paths, rows, points = inner_noise.shape
    groups, dims = lax.axis_size("path"), lax.axis_size("dim")
    inner_total = paths * groups
    zs = groups // 2
    half = zs // 2
    start_row, vol_row, times_row = start[None, :], vol[None, :], times[None, :]
    limit = pltpu.CompilerParams(vmem_limit_bytes=16 * 1024 * 1024)

    lows, held_noise = pl.pallas_call(
        minima_kernel,
        out_shape=(
            pltpu.VMEM((paths, points), F32),
            pltpu.VMEM((rows, paths, points), inner_noise.dtype),
        ),
        in_specs=[pl.BlockSpec(memory_space=pltpu.HBM)] * 5,
        scratch_shapes=[
            pltpu.VMEM((rows, points), outer_noise.dtype),
            pltpu.VMEM((1, rows), F32),
            pltpu.VMEM((1, rows), F32),
            pltpu.VMEM((1, points), F32),
            pltpu.SMEM((1, rows), F32),
            pltpu.VMEM((rows, points), F32),
            pltpu.SemaphoreType.DMA((CHUNKS + 5,)),
        ],
        compiler_params=limit,
        name="minima",
    )(*[
        pltpu.with_memory_space_constraint(x, pltpu.HBM)
        for x in (jnp.transpose(inner_noise, (1, 0, 2)), outer_noise, start_row, vol_row, times_row)
    ])
    held_noise = jnp.transpose(held_noise, (1, 0, 2))

    others = [
        lax.ppermute(lows, "dim", [(i, i ^ s) for i in range(dims)])
        for s in sorted(range(1, dims), key=lambda s: (s < 2, s))
    ]

    parts = pl.pallas_call(
        functools.partial(parts_kernel, zs),
        out_shape=pltpu.VMEM((paths, 2 * zs, LANES, LANES), F32),
        compiler_params=limit,
        cost_estimate=pl.CostEstimate(
            flops=paths * rows * points, bytes_accessed=6 * paths * rows * points, transcendentals=0
        ),
        name="parts",
    )(held_noise)

    send_far, keep_far, keep_near, *send_near = pl.pallas_call(
        functools.partial(moments_kernel, zs, dims),
        out_shape=[pltpu.VMEM((half * LANES + EXTRA, LANES), F32)] * 2
        + [pltpu.VMEM((2 * LANES + EXTRA, LANES), F32)] * half,
        scratch_shapes=[pltpu.VMEM((paths, points), F32), pltpu.VMEM((LANES, LANES), F32)],
        compiler_params=limit,
        name="moments",
    )(lows, *others, parts, times_row)

    def along_z(message, step):
        route = [(i, 2 * owner(i // 2, step, zs) + i % 2) for i in range(groups)]
        return lax.ppermute(message, "path", route)

    def along_y(message):
        return lax.ppermute(message, "path", [(i, i ^ 1) for i in range(groups)])

    messages = pl.pallas_call(
        join_kernel,
        out_shape=[pltpu.VMEM((LANES + EXTRA, LANES), F32)] * half,
        compiler_params=limit,
        name="join",
    )(keep_far, along_y(send_far))
    near_sum = keep_near
    for step in range(1, half):
        near_sum = near_sum + along_z(send_near[step - 1], step)
    scale = pl.pallas_call(
        functools.partial(scale_kernel, inner_total),
        out_shape=pltpu.VMEM((LANES, LANES), F32),
        compiler_params=limit,
        name="scale",
    )(outer_noise, start_row, vol_row, times_row)
    far_extra = messages[0][LANES:]
    arrived = [along_z(message, half + n) for n, message in enumerate(messages)]
    arrived.append(along_y(near_sum[LANES:]))

    value, grad, point, point_grad = pl.pallas_call(
        functools.partial(final_kernel, inner_total, len(arrived)),
        out_shape=[
            jax.ShapeDtypeStruct((1, 1), F32),
            jax.ShapeDtypeStruct((1, rows), F32),
            jax.ShapeDtypeStruct((1, points // groups), F32),
            jax.ShapeDtypeStruct((points // groups, rows), F32),
        ],
        compiler_params=limit,
        name="final",
    )(near_sum, far_extra, scale, outer_noise, start_row, vol_row, times_row, *arrived)
    return value.reshape(1), grad.reshape(rows), point.reshape(points // groups), jnp.transpose(point_grad)


def per_device(inner_noise, outer_noise, start, vol, times):
    rows, points = outer_noise.shape
    groups, dims = lax.axis_size("path"), lax.axis_size("dim")
    fits = (
        2 * points == LANES * groups
        and LANES < rows <= 2 * LANES
        and is_power(groups)
        and groups >= 4
        and is_power(dims)
        and dims > 1
        and points // LANES + 2 <= EXTRA
    )
    return (paired if fits else general)(inner_noise, outer_noise, start, vol, times)


def solution(mesh):
    in_specs = (P("path", "dim", None), P("dim", None), P("dim"), P("dim"), P())
    out_specs = (P(), P("dim"), P("path"), P("dim", "path"))
    return jax.shard_map(
        per_device, mesh=mesh, in_specs=in_specs, out_specs=out_specs, check_vma=False
    )
```
